256 devices in a mesh: row: 16 (over z_lo, x), col: 16 (over z_hi, y, core).
Axes of the slice: x: 4, y: 4, z: 8 (z_hi: 2, z_lo: 4; z = z_hi * 4 + z_lo), core: 2. Of those that a mesh axis runs over, the one named last changes fastest.
Arguments:
- inverse_tiles: bfloat16 [16384, 16384], P('row', 'col'), may hold values from -0.046875 to 0.046875
- factor: bfloat16 [16384, 4, 512], P('row', None, 'col'), may hold values from -0.75 to 0.75
- inverse_diag: float32 [4, 512, 512], P(None, 'row', 'col'), may hold values from -6 to 6
- tile_list: int32 [4, 128], replicated, may hold values from 0 to 127, as said below
- tile_count: int32 [4], replicated, may hold values from 86 to 128, as said below
Outputs:
- inverse_panel: bfloat16 [16384, 4, 512], P(('row', 'col'))
- diag_block: float32 [4, 512, 512], P(None, 'row', 'col')
The draws below stay inside these ranges and needn't reach their ends.
Inputs may be any that keep to these rules, and one draw needn't show every extreme that they name: For each supernode the first tile_count entries of tile_list name distinct tiles in increasing order; the remaining entries name the tiles that are not listed. `tile_count`: some supernode lists all 128 tiles.
All inputs are finite; a program needn't handle non-finite values.
Results may differ from the reference program's by a relative error of at most 0.014.
Values may be sent and summed in bfloat16 or wider, within the bound.
A program may use at most 64 MiB of HBM per device.

```python
import jax
import jax.numpy as jnp
from jax import lax

NS = 4
W = 512
TILE = 128
NA = 16384
NT = 128


def listed_tiles(key):
    base = jax.random.fold_in(key, 7)
    key_pick, key_drop, key_perm = jax.random.split(base, 3)
    complete = jax.random.randint(key_pick, (), 0, NS)
    dropped = jax.random.randint(key_drop, (NS,), 0, NT // 3 + 1)
    dropped = jnp.where(jnp.arange(NS) == complete, 0, dropped)
    counts = (NT - dropped).astype(jnp.int32)
    shuffled = jax.vmap(lambda one_key: jax.random.permutation(one_key, NT))(jax.random.split(key_perm, NS))
    position = jnp.arange(NT, dtype=jnp.int32)[None, :]
    ordering = jnp.where(position < counts[:, None], shuffled, shuffled + NT)
    ordered = jnp.sort(ordering, axis=1)
    ordered = jnp.where(ordered >= NT, ordered - NT, ordered)
    return (ordered.astype(jnp.int32), counts)


def draw_tile_list(key, part):
    return listed_tiles(key)[0]


def draw_tile_count(key, part):
    return listed_tiles(key)[1]


def shard_levels(own_key, shape, cuts, smallest, largest):
    def one(axis_at, parts):
        draws = jax.random.uniform(jax.random.fold_in(jax.random.fold_in(own_key, 6), axis_at), (parts,), jnp.float32, smallest / len(cuts), largest / len(cuts))
        return jnp.repeat(jnp.exp(draws), shape[axis_at] // parts).reshape((-1,) + (1,) * (len(shape) - axis_at - 1))

    loudness = one(*cuts[0])
    for cut in cuts[1:]:
        loudness = loudness * one(*cut)
    return loudness


def bell_draw(stream_key, extent, width, reach, cuts=(), kind=jnp.bfloat16):
    values = jax.random.normal(stream_key, extent, jnp.float32) * width
    if len(cuts) > 0:
        values = shard_levels(stream_key, extent, cuts, -0.22, 0.18) * values
    return jnp.clip(values, min=-reach, max=reach).astype(kind)


def setup_inputs(seed: int = 0) -> dict:
    key_of = jax.random.split(jax.random.key(seed), 6)
    inverse_tiles = bell_draw(key_of[0], (NA, NA), NA ** -0.5, 0.046875, ((0, 16), (1, 16)))
    factor = bell_draw(key_of[1], (NA, NS, W), 64 ** -0.5, 0.75, ((0, 16), (2, 16)))
    inverse_diag = bell_draw(key_of[2], (NS, W, W), 1.0, 6.0, ((1, 16), (2, 16)), jnp.float32)
    tile_list = draw_tile_list(jax.random.fold_in(key_of[5], 71), 0)
    tile_count = draw_tile_count(jax.random.fold_in(key_of[5], 71), 0)
    return {"inverse_tiles": inverse_tiles, "factor": factor, "inverse_diag": inverse_diag, "tile_list": tile_list, "tile_count": tile_count}


def listed_rows(tile_list, tile_count):
    tile_total = tile_list.shape[1]
    position = jnp.arange(tile_total, dtype=jnp.int32)
    matches = (tile_list[:, :, None] == position[None, None, :]) & (position[None, :, None] < tile_count[:, None, None])
    listed = jnp.any(matches, axis=1).astype(jnp.float32)
    return jnp.repeat(listed, TILE, axis=1)


def reference(inverse_tiles, factor, inverse_diag, tile_list, tile_count):
    row_live = listed_rows(tile_list, tile_count).T
    masked = jnp.where(row_live[:, :, None] > 0, factor, jnp.zeros_like(factor))
    product = jnp.dot(inverse_tiles, masked.reshape(NA, NS * W), preferred_element_type=jnp.float32)
    panel_full = -product.reshape(NA, NS, W) * row_live[:, :, None]
    diag_term = jnp.einsum("rsv,rsw->svw", masked.astype(jnp.float32), panel_full, precision=lax.Precision.HIGHEST)
    return panel_full.astype(jnp.bfloat16), inverse_diag - diag_term
```

```python
import jax
import jax.numpy as jnp
from jax import lax
from jax.experimental import pallas as pl
from jax.experimental.pallas import tpu as pltpu
from jax.sharding import PartitionSpec as P

MESH = pl.DeviceIdType.MESH
F32 = jnp.float32
BF16 = jnp.bfloat16
NT_DIMS = (((1,), (1,)), ((), ()))


def div(a, b):
    return lax.div(a, jnp.int32(b))


def rem(a, b):
    return lax.rem(a, jnp.int32(b))


def kernel(
    list_ref, count_ref, a_ref, ft_ref, inv_ref, panel_ref, diag_ref,
    abuf, fmask, fg, fr, pp, pyr, zown, zs, zr, pb, cr, ds, dyr, dxs, dxr, dzs, dzr, perm,
    sems,
):
    row, col = lax.axis_index("row"), lax.axis_index("col")
    zl, x = div(row, 4), rem(row, 4)
    zh, y, k = div(col, 8), rem(div(col, 2), 4), rem(col, 2)
    z, t = zh * 4 + zl, zh * 4 + y

    def at(zl_=zl, x_=x, zh_=zh, y_=y, k_=k):
        return (zl_ * 4 + x_, zh_ * 8 + y_ * 2 + k_)

    used = [0]

    def take(n=1):
        used[0] += n
        return used[0] - n

    def remote(src, dst, send, recv, device):
        return pltpu.make_async_remote_copy(
            src_ref=src, dst_ref=dst, send_sem=sems.at[send], recv_sem=sems.at[recv],
            device_id=device, device_id_type=MESH,
        )

    partner = at(k_=1 - k)
    around_x = [at(x_=rem(x + o, 4)) for o in (1, 2, 3)]
    around_y = [at(y_=rem(y + o, 4)) for o in (1, 2, 3)]
    right, left = around_x[0], around_x[2]

    def chip_t(t_):
        return at(zh_=div(t_, 4), y_=rem(t_, 4))

    def chip_z(z_):
        return at(zh_=div(z_, 4), zl_=rem(z_, 4))

    to_zh, to_y, half = div(zl, 2), rem(zl, 2) * 2 + div(x, 2), rem(x, 2)
    group, place = zh * 2 + div(y, 2), rem(y, 2)
    here = (to_zh == zh) & (to_y == y) & (group == x)

    def source(h, p):
        return at(
            zl_=zh * 2 + div(y, 2), x_=rem(y, 2) * 2 + h, zh_=div(x, 2), y_=rem(x, 2) * 2 + p
        )

    barrier = pltpu.get_barrier_semaphore()

    def greet(device):
        pl.semaphore_signal(barrier, inc=1, device_id=device, device_id_type=MESH)

    greet(partner)
    for device in around_x:
        greet(device)
    for o in range(1, 8):
        greet(chip_t(rem(t + o, 8)))
    for o in range(1, 8):
        if o != 4:
            greet(chip_z(rem(z + o, 8)))
    for h in range(2):
        for p in range(2):
            s_row, s_col = source(h, p)
            same = (s_row == row) & (s_col == col)

            @pl.when(jnp.logical_not(same))
            def _():
                greet((s_row, s_col))

    s_iota = lax.broadcasted_iota(jnp.int32, (4, 128), 0)
    p_iota = lax.broadcasted_iota(jnp.int32, (4, 128), 1)
    counts = jnp.zeros((4, 128), jnp.int32)
    for s in range(4):
        counts = jnp.where(s_iota == s, count_ref[s], counts)
    listed = jnp.where(p_iota < counts, list_ref[...], -1)

    def live(tile):
        return jnp.max(jnp.where(listed == tile, 1.0, 0.0), axis=1, keepdims=True)

    for i in range(8):
        alive = live(row * 8 + i)
        for s in range(4):
            block = ft_ref[s, :, i * 128 : (i + 1) * 128]
            keep = jnp.broadcast_to(alive[s : s + 1, :], block.shape) > 0
            fmask[s, :, i * 128 : (i + 1) * 128] = jnp.where(
                keep, block.astype(F32), 0.0
            ).astype(BF16)
    alive = live(row * 8 + t)
    lane_s = rem(div(lax.broadcasted_iota(jnp.int32, (1, 256), 1), 32), 4)
    lane_live = jnp.zeros((1, 256), F32)
    for s in range(4):
        lane_live = jnp.where(lane_s == s, alive[s : s + 1, :], lane_live)

    pl.semaphore_wait(barrier, 21 - jnp.where(here, 1, 0))

    pending = []

    first_recv = take(4)
    direct = []
    for i in range(4):
        target = at(zl_=rem(zl + i, 4), x_=group, zh_=to_zh, y_=to_y)
        direct.append(
            remote(
                fmask, fg.at[group, half, place], take(), first_recv + half * 2 + place, target
            )
        )
    own_copy = pltpu.make_async_copy(
        fmask, fg.at[group, half, place], sems.at[first_recv + half * 2 + place]
    )

    @pl.when(here)
    def _():
        own_copy.start()

    @pl.when(jnp.logical_not(here))
    def _():
        direct[0].start()

    for copy in direct[1:]:
        copy.start()
    pending += direct[1:]

    a_sems = take(3)
    a_mine = pltpu.make_async_copy(a_ref, abuf.at[k], sems.at[a_sems])
    a_mine.start()
    a_swap = remote(a_ref, abuf.at[k], a_sems + 1, a_sems + 2, partner)
    a_swap.start()
    a_theirs = remote(a_ref, abuf.at[1 - k], a_sems + 1, a_sems + 2, partner)

    def rows_of(t_):
        return fmask.at[:, :, pl.ds(pl.multiple_of(t_ * 128, 128), 128)]

    fr_own_sem = take()
    fr_mine = pltpu.make_async_copy(rows_of(t), fr.at[:, t, k], sems.at[fr_own_sem])
    fr_mine.start()
    fr_arrive = []
    for o in range(1, 8):
        t_to, t_from = rem(t + o, 8), rem(t + 8 - o, 8)
        send, recv = take(), take()
        copy = remote(rows_of(t_to), fr.at[:, t, k], send, recv, chip_t(t_to))
        copy.start()
        pending.append(copy)
        fr_arrive.append(remote(rows_of(t), fr.at[:, t_from, k], send, recv, chip_t(t_from)))

    r_iota = lax.broadcasted_iota(jnp.int32, (256, 512), 0)
    c_iota = lax.broadcasted_iota(jnp.int32, (256, 512), 1)
    same_w = rem(r_iota, 32) == rem(c_iota, 32)
    same_s = rem(div(r_iota, 32), 4) == div(c_iota, 128)
    j4 = rem(div(c_iota, 32), 4)
    for core in range(2):
        hit = same_w & same_s & (j4 == div(r_iota, 128) * 2 + core)
        perm[core] = jnp.where(hit, 1.0, 0.0).astype(BF16)

    g_left, g_right, g_far = rem(x + 3, 4), rem(x + 1, 4), rem(x + 2, 4)
    right_send, right_recv = take(4), take(4)
    left_send, left_recv = take(4), take(4)
    far_right_send, far_right_recv = take(2), take(2)
    far_left_send, far_left_recv = take(2), take(2)
    for p in range(2):
        for h in range(2):
            b = h * 2 + p
            s_dev = source(h, p)
            remote(fmask, fg.at[x, h, p], first_recv, first_recv + b, s_dev).wait_recv()
            block = fg.at[x, h, p]
            for send, recv, device in ((right_send, right_recv, right), (left_send, left_recv, left)):
                copy = remote(block, block, send + b, recv + b, device)
                copy.start()
                pending.append(copy)

    def partial(step, g):
        def body(i, carry):
            rows = pl.ds(pl.multiple_of(i * 256, 256), 256)
            acc = lax.dot_general(
                abuf[0, rows], fg[g, 0].reshape(256, 1024), NT_DIMS, preferred_element_type=F32
            )
            acc += lax.dot_general(
                abuf[1, rows], fg[g, 1].reshape(256, 1024), NT_DIMS, preferred_element_type=F32
            )
            first = rem(i, 2) * 2
            for j in range(2):
                pp[step, div(i, 2), first + j] = acc[j * 128 : (j + 1) * 128].astype(BF16)
            return carry

        lax.fori_loop(0, 4, body, 0)

    y_sems = take(24)
    z_sems, c_sems = take(8), take(8)
    dy_send, dy_recv = take(8), take(8)

    def send_y(step):
        for o in (1, 2, 3):
            sem = y_sems + (step * 3 + o - 1) * 2
            copy = remote(
                pp.at[step, :, rem(y + o, 4)], pyr.at[step, o - 1], sem, sem + 1, around_y[o - 1]
            )
            copy.start()
            pending.append(copy)

    def reduce_y(step):
        for o in (1, 2, 3):
            sem = y_sems + (step * 3 + o - 1) * 2
            came = around_y[3 - o]
            remote(pp.at[step, :, y], pyr.at[step, o - 1], sem, sem + 1, came).wait_recv()

        def total(which):
            acc = pp[step, which, y].astype(F32)
            for o in range(3):
                acc += pyr[step, o, which].astype(F32)
            return acc

        zs[step] = total(1 - zh).astype(BF16)
        copy = remote(
            zs.at[step], zr.at[step], z_sems + step * 2, z_sems + step * 2 + 1, at(zh_=1 - zh)
        )
        copy.start()
        pending.append(copy)
        zown[step] = total(zh)
        return copy

    def finish(step, g, z_copy):
        z_copy.wait_recv()
        panel = -(zown[step] + zr[step].astype(F32))
        panel = jnp.where(lane_live > 0, panel, 0.0)
        pb[step] = panel.astype(BF16)
        theirs = pb.at[step, pl.ds(pl.multiple_of((1 - k) * 64, 64), 64)]
        copy = remote(theirs, cr.at[step], c_sems + step * 2, c_sems + step * 2 + 1, partner)
        copy.start()
        pending.append(copy)
        acc = jnp.zeros((512, 256), F32)
        for s in range(4):
            part = jnp.where(lane_s == s, panel, 0.0).astype(BF16)
            acc += jnp.dot(fr[s].reshape(512, 128), part, preferred_element_type=F32)
        for p in range(2):
            ds[step, p] = acc[:, p * 128 : (p + 1) * 128].astype(BF16)
            y_to, zh_to = rem(g, 2) * 2 + p, div(g, 2)

            @pl.when(y_to == y)
            def _():
                dyr[zh_to, y] = ds[step, p]

            send = remote(
                ds.at[step, p], dyr.at[zh_to, y], dy_send + step * 2 + p,
                dy_recv + zh_to * 4 + y, at(y_=y_to),
            )

            @pl.when(y_to != y)
            def _():
                send.start()

            pending.append((y_to != y, send))
        return copy

    def write_panel(step, g, c_copy):
        c_copy.wait_recv()
        mine = pb[step, pl.ds(pl.multiple_of(k * 64, 64), 64)]
        res = jnp.dot(mine, perm[k], preferred_element_type=F32)
        res += jnp.dot(cr[step], perm[1 - k], preferred_element_type=F32)
        for s in range(4):
            lanes = pl.ds(pl.multiple_of(s * 512 + g * 128, 128), 128)
            panel_ref[:, lanes] = res[:, s * 128 : (s + 1) * 128].astype(BF16)

    a_mine.wait()
    a_theirs.wait_recv()
    pending.append(a_swap)
    partial(0, x)
    send_y(0)

    def came_from_left(h, p):
        b = h * 2 + p
        block = fg.at[g_left, h, p]
        remote(block, block, right_send + b, right_recv + b, left).wait_recv()
        if p == 0:
            copy = remote(block, block, far_right_send + h, far_right_recv + h, right)
            copy.start()
            pending.append(copy)

    def came_from_right(h, p):
        b = h * 2 + p
        block = fg.at[g_right, h, p]
        remote(block, block, left_send + b, left_recv + b, right).wait_recv()
        if p == 1:
            copy = remote(block, block, far_left_send + h, far_left_recv + h, left)
            copy.start()
            pending.append(copy)

    for h in range(2):
        came_from_left(h, 0)
    for h in range(2):
        came_from_right(h, 0)
    for h in range(2):
        came_from_left(h, 1)
        came_from_right(h, 1)
    partial(1, g_left)
    send_y(1)
    partial(2, g_right)
    send_y(2)

    fr_mine.wait()
    for copy in fr_arrive:
        copy.wait_recv()
    fr_sems = take(2)
    fr_swap = remote(fr.at[:, :, k], fr.at[:, :, k], fr_sems, fr_sems + 1, partner)
    fr_swap.start()
    pending.append(fr_swap)
    z0 = reduce_y(0)
    z1 = reduce_y(1)
    z2 = reduce_y(2)
    remote(fr.at[:, :, 1 - k], fr.at[:, :, 1 - k], fr_sems, fr_sems + 1, partner).wait_recv()
    c0 = finish(0, x, z0)
    c1 = finish(1, g_left, z1)
    c2 = finish(2, g_right, z2)

    for h in range(2):
        block = fg.at[g_far, h, 0]
        remote(block, block, far_right_send + h, far_right_recv + h, left).wait_recv()
        block = fg.at[g_far, h, 1]
        remote(block, block, far_left_send + h, far_left_recv + h, right).wait_recv()
    partial(3, g_far)
    send_y(3)
    write_panel(0, x, c0)
    write_panel(1, g_left, c1)
    write_panel(2, g_right, c2)
    z3 = reduce_y(3)
    c3 = finish(3, g_far, z3)
    write_panel(3, g_far, c3)

    for zh_ in range(2):
        for o in (1, 2, 3):
            y_from = rem(y + o, 4)
            remote(
                ds.at[0, 0], dyr.at[zh_, y_from], dy_send, dy_recv + zh_ * 4 + y_from,
                around_y[o - 1],
            ).wait_recv()
    for zh_ in range(2):
        for zl_ in range(4):
            rows = slice(zl_ * 128, (zl_ + 1) * 128)
            acc = dyr[zh_, 0, rows].astype(F32)
            for y_ in range(1, 4):
                acc += dyr[zh_, y_, rows].astype(F32)
            for x_ in range(4):
                dxs[x_, zh_, zl_] = acc[x_ * 32 : (x_ + 1) * 32].astype(BF16)
    arrive = []
    for o in (1, 2, 3):
        send, recv = take(), take()
        copy = remote(dxs.at[rem(x + o, 4)], dxr.at[o - 1], send, recv, around_x[o - 1])
        copy.start()
        pending.append(copy)
        arrive.append(remote(dxs.at[x], dxr.at[o - 1], send, recv, around_x[3 - o]))
    for copy in arrive:
        copy.wait_recv()
    acc = dxs[x].astype(F32)
    for o in range(3):
        acc += dxr[o].astype(F32)
    dzs[...] = acc.astype(BF16)
    arrive = []
    for o in range(1, 8):
        z_to, z_from = rem(z + o, 8), rem(z + 8 - o, 8)
        send, recv = take(), take()
        copy = remote(
            dzs.at[div(z_to, 4), rem(z_to, 4)], dzr.at[o - 1], send, recv, chip_z(z_to)
        )
        copy.start()
        pending.append(copy)
        arrive.append(remote(dzs.at[zh, zl], dzr.at[o - 1], send, recv, chip_z(z_from)))
    for copy in arrive:
        copy.wait_recv()
    total = dzs[zh, zl].astype(F32)
    for o in range(7):
        total += dzr[o].astype(F32)
    for s in range(4):
        diag_ref[s] = inv_ref[s] - total[:, s * 32 : (s + 1) * 32]

    @pl.when(jnp.logical_not(here))
    def _():
        direct[0].wait_send()

    for copy in pending:
        if isinstance(copy, tuple):
            sent, copy = copy
            pl.when(sent)(copy.wait_send)
        else:
            copy.wait_send()
    assert used[0] <= SEMS, used


SEMS = 136


def per_device(inverse_tiles, factor, inverse_diag, tile_list, tile_count):
    vmem = pl.BlockSpec(memory_space=pltpu.VMEM)
    v = pltpu.VMEM
    panel, diag = pl.pallas_call(
        kernel,
        out_shape=(
            jax.ShapeDtypeStruct((64, 2048), BF16),
            jax.ShapeDtypeStruct((4, 32, 32), F32),
        ),
        in_specs=[
            vmem,
            pl.BlockSpec(memory_space=pltpu.SMEM),
            pl.BlockSpec(memory_space=pl.ANY),
            vmem,
            vmem,
        ],
        out_specs=(vmem, vmem),
        scratch_shapes=[
            v((2, 1024, 1024), BF16),
            v((4, 32, 1024), BF16),
            v((4, 2, 2, 4, 32, 1024), BF16),
            v((4, 8, 2, 32, 128), BF16),
            v((4, 2, 4, 128, 256), BF16),
            v((4, 3, 2, 128, 256), BF16),
            v((4, 128, 256), F32),
            v((4, 128, 256), BF16),
            v((4, 128, 256), BF16),
            v((4, 128, 256), BF16),
            v((4, 64, 256), BF16),
            v((4, 2, 512, 128), BF16),
            v((2, 4, 512, 128), BF16),
            v((4, 2, 4, 32, 128), BF16),
            v((3, 2, 4, 32, 128), BF16),
            v((2, 4, 32, 128), BF16),
            v((7, 32, 128), BF16),
            v((2, 256, 512), BF16),
            pltpu.SemaphoreType.DMA((SEMS,)),
        ],
        compiler_params=pltpu.CompilerParams(
            collective_id=0, has_side_effects=True, vmem_limit_bytes=48 * 1024 * 1024
        ),
        cost_estimate=pl.CostEstimate(
            flops=2 * 1024 * 2048 * 1024, bytes_accessed=4 << 20, transcendentals=0
        ),
    )(tile_list, tile_count, inverse_tiles, jnp.transpose(factor, (1, 2, 0)), inverse_diag)
    return panel.reshape(64, 4, 512), diag


def solution(mesh):
    return jax.shard_map(
        per_device,
        mesh=mesh,
        in_specs=(P("row", "col"), P("row", None, "col"), P(None, "row", "col"), P(), P()),
        out_specs=(P(("row", "col"), None, None), P(None, "row", "col")),
        check_vma=False,
    )
```

```python
import jax
import jax.numpy as jnp
from jax import lax
from jax.experimental import pallas as pl
from jax.experimental.pallas import tpu as pltpu
from jax.sharding import PartitionSpec as P

MESH = pl.DeviceIdType.MESH
F32 = jnp.float32
BF16 = jnp.bfloat16
NT_DIMS = (((1,), (1,)), ((), ()))


def div(a, b):
    return lax.div(a, jnp.int32(b))


def rem(a, b):
    return lax.rem(a, jnp.int32(b))


def kernel(
    list_hbm, count_hbm, a_ref, ft_hbm, inv_hbm, panel_ref, diag_ref,
    list_ref, count_ref, ft_ref, inv_ref,
    abuf, fmask, ftile, zbuf, fg, fr, pp, pyr, zown, zs, zr, pb, cr, ds, dyr, dxs, dxr, dzs, dzr,
    perm, spread, sems,
):
    row, col = lax.axis_index("row"), lax.axis_index("col")
    zl, x = div(row, 4), rem(row, 4)
    zh, y, k = div(col, 8), rem(div(col, 2), 4), rem(col, 2)
    z, t = zh * 4 + zl, zh * 4 + y

    def at(zl_=zl, x_=x, zh_=zh, y_=y, k_=k):
        return (zl_ * 4 + x_, zh_ * 8 + y_ * 2 + k_)

    used = [0]

    def take(n=1):
        used[0] += n
        return used[0] - n

    def remote(src, dst, send, recv, device):
        return pltpu.make_async_remote_copy(
            src_ref=src, dst_ref=dst, send_sem=sems.at[send], recv_sem=sems.at[recv],
            device_id=device, device_id_type=MESH,
        )

    partner = at(k_=1 - k)
    around_x = [at(x_=rem(x + o, 4)) for o in (1, 2, 3)]
    around_y = [at(y_=rem(y + o, 4)) for o in (1, 2, 3)]
    right, left = around_x[0], around_x[2]

    def chip_t(t_):
        return at(zh_=div(t_, 4), y_=rem(t_, 4))

    def chip_z(z_, x_=x):
        return at(zh_=div(z_, 4), zl_=rem(z_, 4), x_=x_)

    swap_z = jnp.where((z >= 2) & (z <= 5), 7 - z, z)
    moves = swap_z != z
    across = chip_z(swap_z, rem(x + 2, 4))
    u_own, h_own = div(x, 2), rem(x, 2)

    first = take(5)
    loads = [
        pltpu.make_async_copy(src, dst, sems.at[first + i])
        for i, (src, dst) in enumerate(
            ((ft_hbm, ft_ref), (list_hbm, list_ref), (count_hbm, count_ref), (inv_hbm, inv_ref),
             (a_ref, abuf.at[k]))
        )
    ]
    for copy in loads:
        copy.start()

    barrier = pltpu.get_barrier_semaphore()

    def greet(device):
        pl.semaphore_signal(barrier, inc=1, device_id=device, device_id_type=MESH)

    greet(partner)
    for device in around_x:
        greet(device)
    for o in range(1, 8):
        greet(chip_t(rem(t + o, 8)))
    for o in range(1, 8):
        if o != 4:
            greet(chip_z(rem(z + o, 8)))

    @pl.when(moves)
    def _():
        greet(across)

    for copy in loads[:3]:
        copy.wait()

    s_iota = lax.broadcasted_iota(jnp.int32, (4, 128), 0)
    p_iota = lax.broadcasted_iota(jnp.int32, (4, 128), 1)
    counts = jnp.zeros((4, 128), jnp.int32)
    for s in range(4):
        counts = jnp.where(s_iota == s, count_ref[s], counts)
    listed = jnp.where(p_iota < counts, list_ref[...], -1)

    def live(tile):
        return jnp.max(jnp.where(listed == tile, 1.0, 0.0), axis=1, keepdims=True)

    for i in range(8):
        alive = live(row * 8 + i)
        for s in range(4):
            block = ft_ref[s, :, i * 128 : (i + 1) * 128]
            keep = jnp.broadcast_to(alive[s : s + 1, :], block.shape) > 0
            block = jnp.where(keep, block.astype(F32), 0.0).astype(BF16)
            fmask[s, :, i * 128 : (i + 1) * 128] = block
            ftile[i, s] = block
    alive = live(row * 8 + t)

    pl.semaphore_wait(barrier, 17 + jnp.where(moves, 1, 0))

    pending = []

    hop_send, hop_recv = take(2), take(2)
    kept = fmask.at[pl.ds(u_own * 2, 2)]
    given = fmask.at[pl.ds((1 - u_own) * 2, 2)]
    zl_there = rem(swap_z, 4)
    local_kept = pltpu.make_async_copy(kept, zbuf.at[zl, u_own], sems.at[hop_recv])
    remote_kept = remote(kept, zbuf.at[zl_there, u_own], hop_send, hop_recv, chip_z(swap_z))

    @pl.when(moves)
    def _():
        remote_kept.start()

    @pl.when(jnp.logical_not(moves))
    def _():
        local_kept.start()

    pending.append((moves, remote_kept))
    gift = remote(given, zbuf.at[zl_there, u_own], hop_send + 1, hop_recv + 1, across)
    gift.start()
    pending.append(gift)

    a_sems = take(2)
    a_swap = remote(a_ref, abuf.at[k], a_sems, a_sems + 1, partner)
    a_swap.start()
    pending.append(a_swap)
    a_theirs = remote(a_ref, abuf.at[1 - k], a_sems, a_sems + 1, partner)

    line_send, line_recv = take(6), take(6)

    def held(i):
        if i == 0:
            return zl
        if i == 1:
            return zl + 1 - 2 * rem(zl, 2)
        if i == 2:
            return rem(zl + 2, 4)
        return 3 - zl

    remote(kept, zbuf.at[zl, u_own], hop_send, hop_recv, chip_z(swap_z)).wait_recv()
    remote(given, zbuf.at[zl, 1 - u_own], hop_send + 1, hop_recv + 1, across).wait_recv()
    for i in (1, 2, 3):
        for b in range(2):
            sem = (i - 1) * 2 + b
            copy = remote(
                zbuf.at[zl, b], zbuf.at[zl, b], line_send + sem, line_recv + sem,
                at(zl_=held(i)),
            )
            copy.start()
            pending.append(copy)

    r_iota = lax.broadcasted_iota(jnp.int32, (256, 512), 0)
    c_iota = lax.broadcasted_iota(jnp.int32, (256, 512), 1)
    r_y, r_s, r_w = div(r_iota, 64), rem(div(r_iota, 32), 2), rem(r_iota, 32)
    same_w = r_w == rem(c_iota, 32)
    for core in range(2):
        hit = same_w & (r_s == div(c_iota, 256)) & (div(rem(c_iota, 256), 32) == r_y * 2 + core)
        perm[core] = jnp.where(hit, 1.0, 0.0).astype(BF16)
    for half in range(2):
        hit = same_w & (r_y == div(c_iota, 128)) & (div(rem(c_iota, 128), 32) == half * 2 + r_s)
        spread[half] = jnp.where(hit, 1.0, 0.0).astype(BF16)

    y_send, y_recv = take(8), take(8)
    right_send, right_recv, left_send, left_recv = take(8), take(8), take(8), take(8)
    zh_at = [div(zl, 2), 1 - div(zl, 2)]
    for q in range(2):
        for i in (2 * q, 2 * q + 1):
            place = held(i)
            z_from = zh * 4 + place
            z_from = jnp.where((z_from >= 2) & (z_from <= 5), 7 - z_from, z_from)
            for b in range(2):
                block = zbuf.at[place, b]
                if i > 0:
                    sem = (i - 1) * 2 + b
                    remote(
                        block, block, line_send + sem, line_recv + sem, at(zl_=place)
                    ).wait_recv()
                y_to = rem(z_from, 2) * 2 + b
                there = fg.at[x, zh_at[q], y]
                sem = y_recv + q * 4 + y
                stay = pltpu.make_async_copy(block, there, sems.at[sem])
                send = remote(block, there, y_send + i * 2 + b, sem, at(y_=y_to))

                @pl.when(y_to == y)
                def _():
                    stay.start()

                @pl.when(y_to != y)
                def _():
                    send.start()

                pending.append((y_to != y, send))
        for o in (0, 1, 3, 2):
            y_from = rem(y + o, 4)
            block = fg.at[x, zh_at[q], y_from]
            sem = q * 4 + y_from
            remote(block, block, y_send, y_recv + sem, around_y[o - 1]).wait_recv()
            for send, recv, device in (
                (right_send, right_recv, right), (left_send, left_recv, left)
            ):
                copy = remote(block, block, send + sem, recv + sem, device)
                copy.start()
                pending.append(copy)

    fr_own_sem = take()
    fr_mine = pltpu.make_async_copy(ftile.at[t], fr.at[:, t, k], sems.at[fr_own_sem])
    fr_mine.start()
    fr_arrive = []
    for o in range(1, 8):
        t_to, t_from = rem(t + o, 8), rem(t + 8 - o, 8)
        send, recv = take(), take()
        copy = remote(ftile.at[t_to], fr.at[:, t, k], send, recv, chip_t(t_to))
        copy.start()
        pending.append(copy)
        fr_arrive.append(remote(ftile.at[t], fr.at[:, t_from, k], send, recv, chip_t(t_from)))

    g_left, g_right, g_far = rem(x + 3, 4), rem(x + 1, 4), rem(x + 2, 4)
    far_right_send, far_right_recv = take(4), take(4)
    far_left_send, far_left_recv = take(4), take(4)

    def from_left(q, y_):
        block = fg.at[g_left, zh_at[q], y_]
        sem = q * 4 + y_
        remote(block, block, right_send + sem, right_recv + sem, left).wait_recv()
        if y_ < 2:
            sem = q * 2 + y_
            copy = remote(block, block, far_right_send + sem, far_right_recv + sem, right)
            copy.start()
            pending.append(copy)

    def from_right(q, y_):
        block = fg.at[g_right, zh_at[q], y_]
        sem = q * 4 + y_
        remote(block, block, left_send + sem, left_recv + sem, right).wait_recv()
        if y_ >= 2:
            sem = q * 2 + y_ - 2
            copy = remote(block, block, far_left_send + sem, far_left_recv + sem, left)
            copy.start()
            pending.append(copy)

    def neighbours(q):
        for y_ in range(2):
            from_left(q, y_)
            from_right(q, y_ + 2)
        for y_ in range(2):
            from_left(q, y_ + 2)
            from_right(q, y_)

    def far(q):
        for y_ in range(2):
            sem = q * 2 + y_
            block = fg.at[g_far, zh_at[q], y_]
            remote(block, block, far_right_send + sem, far_right_recv + sem, left).wait_recv()
            block = fg.at[g_far, zh_at[q], y_ + 2]
            remote(block, block, far_left_send + sem, far_left_recv + sem, right).wait_recv()

    u_of = [u_own, u_own, 1 - u_own, 1 - u_own]

    def partial(step):
        u, half = u_of[step], zh_at[step % 2]

        def body(i, carry):
            rows = pl.ds(pl.multiple_of(i * 256, 256), 256)
            acc = lax.dot_general(
                abuf[0, rows], fg[2 * u, half].reshape(256, 1024), NT_DIMS,
                preferred_element_type=F32,
            )
            acc += lax.dot_general(
                abuf[1, rows], fg[2 * u + 1, half].reshape(256, 1024), NT_DIMS,
                preferred_element_type=F32,
            )
            first = rem(i, 2) * 2
            for j in range(2):
                pp[step, div(i, 2), first + j] = acc[j * 128 : (j + 1) * 128].astype(BF16)
            return carry

        lax.fori_loop(0, 4, body, 0)

    y_sems = take(24)
    z_sems, c_sems = take(8), take(8)
    dy_send, dy_recv = take(6), take(8)

    def send_y(step):
        for o in (1, 2, 3):
            sem = y_sems + (step * 3 + o - 1) * 2
            copy = remote(
                pp.at[step, :, rem(y + o, 4)], pyr.at[step, o - 1], sem, sem + 1, around_y[o - 1]
            )
            copy.start()
            pending.append(copy)

    def reduce_y(step):
        for o in (1, 2, 3):
            sem = y_sems + (step * 3 + o - 1) * 2
            came = around_y[3 - o]
            remote(pp.at[step, :, y], pyr.at[step, o - 1], sem, sem + 1, came).wait_recv()

        def total(which):
            acc = pp[step, which, y].astype(F32)
            for o in range(3):
                acc += pyr[step, o, which].astype(F32)
            return acc

        zs[step] = total(1 - zh).astype(BF16)
        copy = remote(
            zs.at[step], zr.at[step], z_sems + step * 2, z_sems + step * 2 + 1, at(zh_=1 - zh)
        )
        copy.start()
        pending.append(copy)
        zown[step] = total(zh)
        return copy

    lane_s = rem(div(lax.broadcasted_iota(jnp.int32, (1, 256), 1), 32), 2)
    wide_s = rem(div(lax.broadcasted_iota(jnp.int32, (1, 512), 1), 32), 2)

    def finish(step, z_copy):
        z_copy.wait_recv()
        s_here = lane_s + 2 * u_of[step]
        lane_live = jnp.zeros((1, 256), F32)
        for s in range(4):
            lane_live = jnp.where(s_here == s, alive[s : s + 1, :], lane_live)
        panel = -(zown[step] + zr[step].astype(F32))
        panel = jnp.where(lane_live > 0, panel, 0.0)
        pb[step] = panel.astype(BF16)
        theirs = pb.at[step, pl.ds(pl.multiple_of((1 - k) * 64, 64), 64)]
        copy = remote(theirs, cr.at[step], c_sems + step * 2, c_sems + step * 2 + 1, partner)
        copy.start()
        pending.append(copy)
        return copy

    def products(pair):
        step, u = pair * 2, u_of[pair * 2]
        panel = jnp.dot(pb[step], spread[zh_at[0]], preferred_element_type=F32)
        panel += jnp.dot(pb[step + 1], spread[zh_at[1]], preferred_element_type=F32)
        acc = jnp.zeros((512, 512), F32)
        for s in range(2):
            part = jnp.where(wide_s == s, panel, 0.0).astype(BF16)
            acc += jnp.dot(fr[2 * u + s].reshape(512, 128), part, preferred_element_type=F32)
        for y_ in range(4):
            ds[pair, y_] = acc[:, y_ * 128 : (y_ + 1) * 128].astype(BF16)
        for o in (1, 3, 2):
            send = remote(
                ds.at[pair, rem(y + o, 4)], dyr.at[u, y], dy_send + pair * 3 + o - 1,
                dy_recv + u * 4 + y, around_y[o - 1],
            )
            send.start()
            pending.append(send)
        dyr[u, y] = ds[pair, y]

    def write_panel(step, c_copy):
        c_copy.wait_recv()
        mine = pb[step, pl.ds(pl.multiple_of(k * 64, 64), 64)]
        res = jnp.dot(mine, perm[k], preferred_element_type=F32)
        res += jnp.dot(cr[step], perm[1 - k], preferred_element_type=F32)
        for s in range(2):
            lane = (2 * u_of[step] + s) * 512 + zh_at[step % 2] * 256
            panel_ref[:, pl.ds(pl.multiple_of(lane, 256), 256)] = res[
                :, s * 256 : (s + 1) * 256
            ].astype(BF16)

    neighbours(0)
    loads[4].wait()
    a_theirs.wait_recv()
    partial(0)
    send_y(0)
    neighbours(1)
    partial(1)
    send_y(1)
    z0 = reduce_y(0)

    fr_mine.wait()
    for copy in fr_arrive:
        copy.wait_recv()
    fr_sems = take(2)
    fr_swap = remote(fr.at[:, :, k], fr.at[:, :, k], fr_sems, fr_sems + 1, partner)
    fr_swap.start()
    pending.append(fr_swap)

    far(0)
    partial(2)
    send_y(2)
    z1 = reduce_y(1)
    c0 = finish(0, z0)
    far(1)
    partial(3)
    send_y(3)
    z2 = reduce_y(2)
    c1 = finish(1, z1)
    remote(fr.at[:, :, 1 - k], fr.at[:, :, 1 - k], fr_sems, fr_sems + 1, partner).wait_recv()
    products(0)
    z3 = reduce_y(3)
    write_panel(0, c0)
    write_panel(1, c1)
    c2 = finish(2, z2)
    c3 = finish(3, z3)
    products(1)
    write_panel(2, c2)
    write_panel(3, c3)

    def over_y(u):
        for o in (1, 3, 2):
            y_from = rem(y + o, 4)
            remote(
                ds.at[0, 0], dyr.at[u, y_from], dy_send, dy_recv + u * 4 + y_from,
                around_y[o - 1],
            ).wait_recv()
        for zl_ in range(4):
            rows = slice(zl_ * 128, (zl_ + 1) * 128)
            acc = dyr[u, 0, rows].astype(F32)
            for y_ in range(1, 4):
                acc += dyr[u, y_, rows].astype(F32)
            for x_ in range(4):
                dxs[x_, u, zl_] = acc[x_ * 32 : (x_ + 1) * 32].astype(BF16)

    over_y(u_own)
    over_y(1 - u_own)
    arrive = []
    for o in (1, 3, 2):
        send, recv = take(), take()
        copy = remote(dxs.at[rem(x + o, 4)], dxr.at[o - 1], send, recv, around_x[o - 1])
        copy.start()
        pending.append(copy)
        arrive.append(remote(dxs.at[x], dxr.at[o - 1], send, recv, around_x[3 - o]))
    for copy in arrive:
        copy.wait_recv()
    acc = dxs[x].astype(F32)
    for o in range(3):
        acc += dxr[o].astype(F32)
    for zl_ in range(4):
        dzs[zl_] = acc[:, zl_].astype(BF16)
    arrive = []
    for o in (4, 3, 5, 2, 6, 1, 7):
        z_to, z_from = rem(z + o, 8), rem(z + 8 - o, 8)
        send, recv = take(), take()
        copy = remote(dzs.at[rem(z_to, 4)], dzr.at[o - 1], send, recv, chip_z(z_to))
        copy.start()
        pending.append(copy)
        arrive.append(remote(dzs.at[zl], dzr.at[o - 1], send, recv, chip_z(z_from)))
    for copy in arrive:
        copy.wait_recv()
    total = dzs[zl].astype(F32)
    for o in range(7):
        total += dzr[o].astype(F32)
    total = jnp.where(zh == 0, total[:, :, :64], total[:, :, 64:])
    loads[3].wait()
    for s in range(4):
        diag_ref[s] = inv_ref[s] - total[s // 2, :, (s % 2) * 32 : (s % 2 + 1) * 32]

    for copy in pending:
        if isinstance(copy, tuple):
            sent, copy = copy
            pl.when(sent)(copy.wait_send)
        else:
            copy.wait_send()
    assert used[0] <= SEMS, used


SEMS = 208


def per_device(inverse_tiles, factor, inverse_diag, tile_list, tile_count):
    vmem = pl.BlockSpec(memory_space=pltpu.VMEM)
    v = pltpu.VMEM
    panel, diag = pl.pallas_call(
        kernel,
        out_shape=(
            jax.ShapeDtypeStruct((64, 2048), BF16),
            jax.ShapeDtypeStruct((4, 32, 32), F32),
        ),
        in_specs=[pl.BlockSpec(memory_space=pl.ANY)] * 5,
        out_specs=(vmem, vmem),
        scratch_shapes=[
            v((4, 128), jnp.int32),
            pltpu.SMEM((4,), jnp.int32),
            v((4, 32, 1024), BF16),
            v((4, 32, 32), F32),
            v((2, 1024, 1024), BF16),
            v((4, 32, 1024), BF16),
            v((8, 4, 32, 128), BF16),
            v((4, 2, 2, 32, 1024), BF16),
            v((4, 2, 4, 2, 32, 1024), BF16),
            v((4, 8, 2, 32, 128), BF16),
            v((4, 2, 4, 128, 256), BF16),
            v((4, 3, 2, 128, 256), BF16),
            v((4, 128, 256), F32),
            v((4, 128, 256), BF16),
            v((4, 128, 256), BF16),
            v((4, 128, 256), BF16),
            v((4, 64, 256), BF16),
            v((2, 4, 512, 128), BF16),
            v((2, 4, 512, 128), BF16),
            v((4, 2, 4, 32, 128), BF16),
            v((3, 2, 4, 32, 128), BF16),
            v((4, 2, 32, 128), BF16),
            v((7, 2, 32, 128), BF16),
            v((2, 256, 512), BF16),
            v((2, 256, 512), BF16),
            pltpu.SemaphoreType.DMA((SEMS,)),
        ],
        compiler_params=pltpu.CompilerParams(
            collective_id=0, has_side_effects=True, vmem_limit_bytes=60 * 1024 * 1024
        ),
        cost_estimate=pl.CostEstimate(
            flops=2 * 1024 * 2048 * 1024, bytes_accessed=4 << 20, transcendentals=0
        ),
    )(tile_list, tile_count, inverse_tiles, jnp.transpose(factor, (1, 2, 0)), inverse_diag)
    return panel.reshape(64, 4, 512), diag


def solution(mesh):
    return jax.shard_map(
        per_device,
        mesh=mesh,
        in_specs=(P("row", "col"), P("row", None, "col"), P(None, "row", "col"), P(), P()),
        out_specs=(P(("row", "col"), None, None), P(None, "row", "col")),
        check_vma=False,
    )
```

```python
import jax
import jax.numpy as jnp
from jax import lax
from jax.experimental import pallas as pl
from jax.experimental.pallas import tpu as pltpu
from jax.sharding import PartitionSpec as P

MESH = pl.DeviceIdType.MESH
F32 = jnp.float32
BF16 = jnp.bfloat16
NT_DIMS = (((1,), (1,)), ((), ()))


def div(a, b):
    return lax.div(a, jnp.int32(b))


def rem(a, b):
    return lax.rem(a, jnp.int32(b))


def kernel(
    list_hbm, count_hbm, a_ref, ft_hbm, inv_hbm, panel_ref, diag_ref,
    list_ref, count_ref, ft_ref, inv_ref,
    abuf, fmask, ftile, fg, fr, pp, pyr, zown, zs, zr, pb, cr, ds, dyr, dxs, dxr, dzs, dzr,
    perm, spread, sems,
):
    row, col = lax.axis_index("row"), lax.axis_index("col")
    zl, x = div(row, 4), rem(row, 4)
    zh, y, k = div(col, 8), rem(div(col, 2), 4), rem(col, 2)
    z, t = zh * 4 + zl, zh * 4 + y

    def at(zl_=zl, x_=x, zh_=zh, y_=y, k_=k):
        return (zl_ * 4 + x_, zh_ * 8 + y_ * 2 + k_)

    used = [0]

    def take(n=1):
        used[0] += n
        return used[0] - n

    def remote(src, dst, send, recv, device):
        return pltpu.make_async_remote_copy(
            src_ref=src, dst_ref=dst, send_sem=sems.at[send], recv_sem=sems.at[recv],
            device_id=device, device_id_type=MESH,
        )

    partner = at(k_=1 - k)
    around_x = [at(x_=rem(x + o, 4)) for o in (1, 2, 3)]
    around_y = [at(y_=rem(y + o, 4)) for o in (1, 2, 3)]
    right, left = around_x[0], around_x[2]

    def chip_t(t_):
        return at(zh_=div(t_, 4), y_=rem(t_, 4))

    def chip_z(z_, x_=x):
        return at(zh_=div(z_, 4), zl_=rem(z_, 4), x_=x_)

    u_own = div(x, 2)
    to_zh, to_y = div(zl, 2), rem(zl, 2) * 2 + div(x, 2)
    to_place, to_yh = zh * 2 + rem(y, 2), div(y, 2)
    here = (to_zh == zh) & (to_y == y) & (to_place == zl)

    def source(yh):
        return at(
            x_=jnp.where(u_own == rem(y, 2), x, rem(x + 2, 4)), y_=yh * 2 + rem(zl, 2),
            zh_=div(zl, 2), zl_=zh * 2 + div(y, 2),
        )

    first = take(5)
    loads = [
        pltpu.make_async_copy(src, dst, sems.at[first + i])
        for i, (src, dst) in enumerate(
            ((ft_hbm, ft_ref), (list_hbm, list_ref), (count_hbm, count_ref), (inv_hbm, inv_ref),
             (a_ref, abuf.at[k]))
        )
    ]
    for copy in loads:
        copy.start()

    barrier = pltpu.get_barrier_semaphore()

    def greet(device):
        pl.semaphore_signal(barrier, inc=1, device_id=device, device_id_type=MESH)

    greet(partner)
    for device in around_x:
        greet(device)
    for o in range(1, 8):
        greet(chip_t(rem(t + o, 8)))
    for o in range(1, 8):
        if o != 4:
            greet(chip_z(rem(z + o, 8)))

    for yh in range(2):
        s_row, s_col = source(yh)

        @pl.when((s_row != row) | (s_col != col))
        def _():
            greet((s_row, s_col))

    for copy in loads[:3]:
        copy.wait()

    s_iota = lax.broadcasted_iota(jnp.int32, (4, 128), 0)
    p_iota = lax.broadcasted_iota(jnp.int32, (4, 128), 1)
    counts = jnp.zeros((4, 128), jnp.int32)
    for s in range(4):
        counts = jnp.where(s_iota == s, count_ref[s], counts)
    listed = jnp.where(p_iota < counts, list_ref[...], -1)

    def live(tile):
        return jnp.max(jnp.where(listed == tile, 1.0, 0.0), axis=1, keepdims=True)

    for i in range(8):
        alive = live(row * 8 + i)
        for s in range(4):
            block = ft_ref[s, :, i * 128 : (i + 1) * 128]
            keep = jnp.broadcast_to(alive[s : s + 1, :], block.shape) > 0
            block = jnp.where(keep, block.astype(F32), 0.0).astype(BF16)
            fmask[s, :, i * 128 : (i + 1) * 128] = block
            ftile[i, s] = block
    alive = live(row * 8 + t)

    pl.semaphore_wait(barrier, 19 - jnp.where(here, 1, 0))

    pending = []

    hop_send, hop_recv = take(2), take(2)
    kept = fmask.at[pl.ds(u_own * 2, 2)]
    given = fmask.at[pl.ds((1 - u_own) * 2, 2)]
    across = rem(x + 2, 4)
    gift = remote(
        given, fg.at[across, to_place, to_yh], hop_send + 1, hop_recv + to_yh,
        at(x_=across, y_=to_y, zh_=to_zh, zl_=to_place),
    )
    gift.start()
    pending.append(gift)
    there = fg.at[x, to_place, to_yh]
    local_kept = pltpu.make_async_copy(kept, there, sems.at[hop_recv + to_yh])
    remote_kept = remote(
        kept, there, hop_send, hop_recv + to_yh, at(y_=to_y, zh_=to_zh, zl_=to_place)
    )

    @pl.when(here)
    def _():
        local_kept.start()

    @pl.when(jnp.logical_not(here))
    def _():
        remote_kept.start()

    pending.append((jnp.logical_not(here), remote_kept))

    a_sems = take(2)
    a_swap = remote(a_ref, abuf.at[k], a_sems, a_sems + 1, partner)
    a_swap.start()
    pending.append(a_swap)
    a_theirs = remote(a_ref, abuf.at[1 - k], a_sems, a_sems + 1, partner)

    r_iota = lax.broadcasted_iota(jnp.int32, (256, 512), 0)
    c_iota = lax.broadcasted_iota(jnp.int32, (256, 512), 1)
    r_y = rem(div(r_iota, 64), 2) * 2 + div(r_iota, 128)
    r_s, r_w = rem(div(r_iota, 32), 2), rem(r_iota, 32)
    same_w = r_w == rem(c_iota, 32)
    for core in range(2):
        hit = same_w & (r_s == div(c_iota, 256)) & (div(rem(c_iota, 256), 32) == r_y * 2 + core)
        perm[core] = jnp.where(hit, 1.0, 0.0).astype(BF16)
    for half in range(2):
        hit = same_w & (r_y == div(c_iota, 128)) & (div(rem(c_iota, 128), 32) == half * 2 + r_s)
        spread[half] = jnp.where(hit, 1.0, 0.0).astype(BF16)

    line_send, line_recv, pass_send = take(2), take(4), take(3)
    right_send, right_recv, left_send, left_recv = take(4), take(4), take(4), take(4)
    zh_at = [div(zl, 2), 1 - div(zl, 2)]
    inner = (zl == 1) | (zl == 2)
    even = rem(zl, 2) == 0
    flip1 = jnp.where(even, zl + 1, zl - 1)
    flip2 = rem(zl + 2, 4)
    flip3 = 3 - zl
    order = [zl, flip1, jnp.where(inner, flip3, flip2), jnp.where(inner, flip2, flip3)]

    def along_line(place, sem, to):
        on = (to >= 0) & (to <= 3)
        block = fg.at[x, place]
        copy = remote(block, block, sem, line_recv + place, at(zl_=jnp.clip(to, 0, 3)))
        pl.when(on)(copy.start)
        pending.append((on, copy))

    def along_x(place):
        block = fg.at[x, place]
        for send, recv, device in (
            (right_send, right_recv, right), (left_send, left_recv, left)
        ):
            copy = remote(block, block, send + place, recv + place, device)
            copy.start()
            pending.append(copy)

    for yh in range(2):
        remote(
            kept, fg.at[x, zl, yh], hop_send, hop_recv + yh, around_x[0]
        ).wait_recv()
    along_line(zl, line_send, zl + 1)
    along_line(zl, line_send + 1, zl - 1)
    along_x(zl)
    for i in (1, 2, 3):
        place = order[i]
        block = fg.at[x, place]
        remote(block, block, line_send, line_recv + place, around_x[0]).wait_recv()
        along_line(place, pass_send + i - 1, jnp.where(place > zl, zl - 1, zl + 1))
        along_x(place)

    fr_own_sem = take()
    fr_mine = pltpu.make_async_copy(ftile.at[t], fr.at[:, t, k], sems.at[fr_own_sem])
    fr_mine.start()
    fr_arrive = []
    for o in range(1, 8):
        t_to, t_from = rem(t + o, 8), rem(t + 8 - o, 8)
        send, recv = take(), take()
        copy = remote(ftile.at[t_to], fr.at[:, t, k], send, recv, chip_t(t_to))
        copy.start()
        pending.append(copy)
        fr_arrive.append(remote(ftile.at[t], fr.at[:, t_from, k], send, recv, chip_t(t_from)))

    g_left, g_right, g_far = rem(x + 3, 4), rem(x + 1, 4), rem(x + 2, 4)
    far_right_send, far_right_recv = take(4), take(4)
    far_left_send, far_left_recv = take(4), take(4)

    def neighbours(i):
        place = order[i]
        for sems_at, group, half, onward, device, back in (
            ((right_send, right_recv), g_left, 0, (far_right_send, far_right_recv), right, left),
            ((left_send, left_recv), g_right, 1, (far_left_send, far_left_recv), left, right),
        ):
            block = fg.at[group, place]
            remote(block, block, sems_at[0] + place, sems_at[1] + place, back).wait_recv()
            part = fg.at[group, place, half]
            copy = remote(part, part, onward[0] + place, onward[1] + place, device)
            copy.start()
            pending.append(copy)

    def far(i):
        place = order[i]
        part = fg.at[g_far, place, 0]
        remote(part, part, far_right_send, far_right_recv + place, left).wait_recv()
        part = fg.at[g_far, place, 1]
        remote(part, part, far_left_send, far_left_recv + place, right).wait_recv()

    u_of = [u_own, u_own, 1 - u_own, 1 - u_own]

    def partial(step):
        u, half = u_of[step], zh_at[step % 2]

        def body(i, carry):
            rows = pl.ds(pl.multiple_of(i * 256, 256), 256)
            acc = lax.dot_general(
                abuf[0, rows], fg[2 * u, pl.ds(2 * half, 2)].reshape(256, 1024), NT_DIMS,
                preferred_element_type=F32,
            )
            acc += lax.dot_general(
                abuf[1, rows], fg[2 * u + 1, pl.ds(2 * half, 2)].reshape(256, 1024), NT_DIMS,
                preferred_element_type=F32,
            )
            first = rem(i, 2) * 2
            for j in range(2):
                pp[step, div(i, 2), first + j] = acc[j * 128 : (j + 1) * 128].astype(BF16)
            return carry

        lax.fori_loop(0, 4, body, 0)

    y_sems = take(24)
    z_sems, c_sems = take(8), take(8)
    dy_send, dy_recv = take(6), take(8)

    def send_y(step):
        for o in (1, 2, 3):
            sem = y_sems + (step * 3 + o - 1) * 2
            copy = remote(
                pp.at[step, :, rem(y + o, 4)], pyr.at[step, o - 1], sem, sem + 1, around_y[o - 1]
            )
            copy.start()
            pending.append(copy)

    def reduce_y(step):
        for o in (1, 2, 3):
            sem = y_sems + (step * 3 + o - 1) * 2
            came = around_y[3 - o]
            remote(pp.at[step, :, y], pyr.at[step, o - 1], sem, sem + 1, came).wait_recv()

        def total(which):
            acc = pp[step, which, y].astype(F32)
            for o in range(3):
                acc += pyr[step, o, which].astype(F32)
            return acc

        zs[step] = total(1 - zh).astype(BF16)
        copy = remote(
            zs.at[step], zr.at[step], z_sems + step * 2, z_sems + step * 2 + 1, at(zh_=1 - zh)
        )
        copy.start()
        pending.append(copy)
        zown[step] = total(zh)
        return copy

    lane_s = rem(div(lax.broadcasted_iota(jnp.int32, (1, 256), 1), 32), 2)
    wide_s = rem(div(lax.broadcasted_iota(jnp.int32, (1, 512), 1), 32), 2)

    def finish(step, z_copy):
        z_copy.wait_recv()
        s_here = lane_s + 2 * u_of[step]
        lane_live = jnp.zeros((1, 256), F32)
        for s in range(4):
            lane_live = jnp.where(s_here == s, alive[s : s + 1, :], lane_live)
        panel = -(zown[step] + zr[step].astype(F32))
        panel = jnp.where(lane_live > 0, panel, 0.0)
        pb[step] = panel.astype(BF16)
        theirs = pb.at[step, pl.ds(pl.multiple_of((1 - k) * 64, 64), 64)]
        copy = remote(theirs, cr.at[step], c_sems + step * 2, c_sems + step * 2 + 1, partner)
        copy.start()
        pending.append(copy)
        return copy

    def products(pair):
        step, u = pair * 2, u_of[pair * 2]
        panel = jnp.dot(pb[step], spread[zh_at[0]], preferred_element_type=F32)
        panel += jnp.dot(pb[step + 1], spread[zh_at[1]], preferred_element_type=F32)
        acc = jnp.zeros((512, 512), F32)
        for s in range(2):
            part = jnp.where(wide_s == s, panel, 0.0).astype(BF16)
            acc += jnp.dot(fr[2 * u + s].reshape(512, 128), part, preferred_element_type=F32)
        for y_ in range(4):
            ds[pair, y_] = acc[:, y_ * 128 : (y_ + 1) * 128].astype(BF16)
        for o in (1, 3, 2):
            send = remote(
                ds.at[pair, rem(y + o, 4)], dyr.at[u, y], dy_send + pair * 3 + o - 1,
                dy_recv + u * 4 + y, around_y[o - 1],
            )
            send.start()
            pending.append(send)
        dyr[u, y] = ds[pair, y]

    def write_panel(step, c_copy):
        c_copy.wait_recv()
        mine = pb[step, pl.ds(pl.multiple_of(k * 64, 64), 64)]
        res = jnp.dot(mine, perm[k], preferred_element_type=F32)
        res += jnp.dot(cr[step], perm[1 - k], preferred_element_type=F32)
        for s in range(2):
            lane = (2 * u_of[step] + s) * 512 + zh_at[step % 2] * 256
            panel_ref[:, pl.ds(pl.multiple_of(lane, 256), 256)] = res[
                :, s * 256 : (s + 1) * 256
            ].astype(BF16)

    neighbours(0)
    neighbours(1)
    loads[4].wait()
    a_theirs.wait_recv()
    partial(0)
    send_y(0)
    neighbours(2)
    fr_mine.wait()
    for copy in fr_arrive:
        copy.wait_recv()
    fr_sems = take(2)
    fr_swap = remote(fr.at[:, :, k], fr.at[:, :, k], fr_sems, fr_sems + 1, partner)
    fr_swap.start()
    pending.append(fr_swap)
    z0 = reduce_y(0)
    neighbours(3)
    partial(1)
    send_y(1)
    far(0)
    far(1)
    partial(2)
    send_y(2)
    z1 = reduce_y(1)
    c0 = finish(0, z0)
    remote(fr.at[:, :, 1 - k], fr.at[:, :, 1 - k], fr_sems, fr_sems + 1, partner).wait_recv()
    c1 = finish(1, z1)
    products(0)
    z2 = reduce_y(2)
    far(2)
    far(3)
    partial(3)
    send_y(3)
    write_panel(0, c0)
    write_panel(1, c1)
    c2 = finish(2, z2)
    z3 = reduce_y(3)
    write_panel(2, c2)
    c3 = finish(3, z3)
    products(1)
    write_panel(3, c3)

    def over_y(u):
        for o in (1, 3, 2):
            y_from = rem(y + o, 4)
            remote(
                ds.at[0, 0], dyr.at[u, y_from], dy_send, dy_recv + u * 4 + y_from,
                around_y[o - 1],
            ).wait_recv()
        for zl_ in range(4):
            rows = slice(zl_ * 128, (zl_ + 1) * 128)
            acc = dyr[u, 0, rows].astype(F32)
            for y_ in range(1, 4):
                acc += dyr[u, y_, rows].astype(F32)
            for x_ in range(4):
                dxs[x_, u, zl_] = acc[x_ * 32 : (x_ + 1) * 32].astype(BF16)

    over_y(u_own)
    over_y(1 - u_own)
    arrive = []
    for o in (1, 3, 2):
        send, recv = take(), take()
        copy = remote(dxs.at[rem(x + o, 4)], dxr.at[o - 1], send, recv, around_x[o - 1])
        copy.start()
        pending.append(copy)
        arrive.append(remote(dxs.at[x], dxr.at[o - 1], send, recv, around_x[3 - o]))
    for copy in arrive:
        copy.wait_recv()
    acc = dxs[x].astype(F32)
    for o in range(3):
        acc += dxr[o].astype(F32)
    for zl_ in range(4):
        dzs[zl_] = acc[:, zl_].astype(BF16)
    arrive = []
    for o in (4, 3, 5, 2, 6, 1, 7):
        z_to, z_from = rem(z + o, 8), rem(z + 8 - o, 8)
        send, recv = take(), take()
        copy = remote(dzs.at[rem(z_to, 4)], dzr.at[o - 1], send, recv, chip_z(z_to))
        copy.start()
        pending.append(copy)
        arrive.append(remote(dzs.at[zl], dzr.at[o - 1], send, recv, chip_z(z_from)))
    for copy in arrive:
        copy.wait_recv()
    total = dzs[zl].astype(F32)
    for o in range(7):
        total += dzr[o].astype(F32)
    total = jnp.where(zh == 0, total[:, :, :64], total[:, :, 64:])
    loads[3].wait()
    for s in range(4):
        diag_ref[s] = inv_ref[s] - total[s // 2, :, (s % 2) * 32 : (s % 2 + 1) * 32]

    for copy in pending:
        if isinstance(copy, tuple):
            sent, copy = copy
            pl.when(sent)(copy.wait_send)
        else:
            copy.wait_send()
    assert used[0] <= SEMS, used


SEMS = 208


def per_device(inverse_tiles, factor, inverse_diag, tile_list, tile_count):
    vmem = pl.BlockSpec(memory_space=pltpu.VMEM)
    v = pltpu.VMEM
    panel, diag = pl.pallas_call(
        kernel,
        out_shape=(
            jax.ShapeDtypeStruct((64, 2048), BF16),
            jax.ShapeDtypeStruct((4, 32, 32), F32),
        ),
        in_specs=[pl.BlockSpec(memory_space=pl.ANY)] * 5,
        out_specs=(vmem, vmem),
        scratch_shapes=[
            v((4, 128), jnp.int32),
            pltpu.SMEM((4,), jnp.int32),
            v((4, 32, 1024), BF16),
            v((4, 32, 32), F32),
            v((2, 1024, 1024), BF16),
            v((4, 32, 1024), BF16),
            v((8, 4, 32, 128), BF16),
            v((4, 4, 2, 2, 32, 1024), BF16),
            v((4, 8, 2, 32, 128), BF16),
            v((4, 2, 4, 128, 256), BF16),
            v((4, 3, 2, 128, 256), BF16),
            v((4, 128, 256), F32),
            v((4, 128, 256), BF16),
            v((4, 128, 256), BF16),
            v((4, 128, 256), BF16),
            v((4, 64, 256), BF16),
            v((2, 4, 512, 128), BF16),
            v((2, 4, 512, 128), BF16),
            v((4, 2, 4, 32, 128), BF16),
            v((3, 2, 4, 32, 128), BF16),
            v((4, 2, 32, 128), BF16),
            v((7, 2, 32, 128), BF16),
            v((2, 256, 512), BF16),
            v((2, 256, 512), BF16),
            pltpu.SemaphoreType.DMA((SEMS,)),
        ],
        compiler_params=pltpu.CompilerParams(
            collective_id=0, has_side_effects=True, vmem_limit_bytes=60 * 1024 * 1024
        ),
        cost_estimate=pl.CostEstimate(
            flops=2 * 1024 * 2048 * 1024, bytes_accessed=4 << 20, transcendentals=0
        ),
    )(tile_list, tile_count, inverse_tiles, jnp.transpose(factor, (1, 2, 0)), inverse_diag)
    return panel.reshape(64, 4, 512), diag


def solution(mesh):
    return jax.shard_map(
        per_device,
        mesh=mesh,
        in_specs=(P("row", "col"), P("row", None, "col"), P(None, "row", "col"), P(), P()),
        out_specs=(P(("row", "col"), None, None), P(None, "row", "col")),
        check_vma=False,
    )
```

```python
import jax
import jax.numpy as jnp
from jax import lax
from jax.experimental import pallas as pl
from jax.experimental.pallas import tpu as pltpu
from jax.sharding import PartitionSpec as P

MESH = pl.DeviceIdType.MESH
F32 = jnp.float32
BF16 = jnp.bfloat16
NT_DIMS = (((1,), (1,)), ((), ()))


def div(a, b):
    return lax.div(a, jnp.int32(b))


def rem(a, b):
    return lax.rem(a, jnp.int32(b))


def kernel(
    list_hbm, count_hbm, a_ref, ft_hbm, inv_hbm, panel_ref, diag_ref,
    list_ref, count_ref, ft_ref, inv_ref,
    abuf, fmask, ftile, fg, fr, pp, pyr, sb, zown, zs, zr, pb, cr, ds, dyr, dxs, dxr, dzs,
    dzr, perm, sems,
):
    row, col = lax.axis_index("row"), lax.axis_index("col")
    zl, x = div(row, 4), rem(row, 4)
    zh, y, k = div(col, 8), rem(div(col, 2), 4), rem(col, 2)
    z, t = zh * 4 + zl, zh * 4 + y

    def at(zl_=zl, x_=x, zh_=zh, y_=y, k_=k):
        return (zl_ * 4 + x_, zh_ * 8 + y_ * 2 + k_)

    used = [0]

    def take(n=1):
        used[0] += n
        return used[0] - n

    def remote(src, dst, send, recv, device):
        return pltpu.make_async_remote_copy(
            src_ref=src, dst_ref=dst, send_sem=sems.at[send], recv_sem=sems.at[recv],
            device_id=device, device_id_type=MESH,
        )

    partner = at(k_=1 - k)
    around_x = [at(x_=rem(x + o, 4)) for o in (1, 2, 3)]
    around_y = [at(y_=rem(y + o, 4)) for o in (1, 2, 3)]
    right, left = around_x[0], around_x[2]

    def chip_t(t_):
        return at(zh_=div(t_, 4), y_=rem(t_, 4))

    def chip_z(z_, x_=x):
        return at(zh_=div(z_, 4), zl_=rem(z_, 4), x_=x_)

    u_own = div(x, 2)
    to_zh, to_y = div(zl, 2), rem(zl, 2) * 2 + div(x, 2)
    to_place, to_yh = zh * 2 + rem(y, 2), div(y, 2)
    here = (to_zh == zh) & (to_y == y) & (to_place == zl)

    def source(yh):
        return at(
            x_=jnp.where(u_own == rem(y, 2), x, rem(x + 2, 4)), y_=yh * 2 + rem(zl, 2),
            zh_=div(zl, 2), zl_=zh * 2 + div(y, 2),
        )

    first = take(5)
    loads = [
        pltpu.make_async_copy(src, dst, sems.at[first + i])
        for i, (src, dst) in enumerate(
            ((ft_hbm, ft_ref), (list_hbm, list_ref), (count_hbm, count_ref), (inv_hbm, inv_ref),
             (a_ref, abuf.at[k]))
        )
    ]
    for copy in loads:
        copy.start()

    barrier = pltpu.get_barrier_semaphore()

    def greet(device):
        pl.semaphore_signal(barrier, inc=1, device_id=device, device_id_type=MESH)

    greet(partner)
    for device in around_x:
        greet(device)
    for o in range(1, 8):
        greet(chip_t(rem(t + o, 8)))
    for o in range(1, 8):
        if o != 4:
            greet(chip_z(rem(z + o, 8)))

    for yh in range(2):
        s_row, s_col = source(yh)

        @pl.when((s_row != row) | (s_col != col))
        def _():
            greet((s_row, s_col))

    for copy in loads[:3]:
        copy.wait()

    s_iota = lax.broadcasted_iota(jnp.int32, (4, 128), 0)
    p_iota = lax.broadcasted_iota(jnp.int32, (4, 128), 1)
    counts = jnp.zeros((4, 128), jnp.int32)
    for s in range(4):
        counts = jnp.where(s_iota == s, count_ref[s], counts)
    listed = jnp.where(p_iota < counts, list_ref[...], -1)

    def live(tile):
        return jnp.max(jnp.where(listed == tile, 1.0, 0.0), axis=1, keepdims=True)

    for i in range(8):
        alive = live(row * 8 + i)
        for s in range(4):
            block = ft_ref[s, :, i * 128 : (i + 1) * 128]
            keep = jnp.broadcast_to(alive[s : s + 1, :], block.shape) > 0
            block = jnp.where(keep, block.astype(F32), 0.0).astype(BF16)
            fmask[s, :, i * 128 : (i + 1) * 128] = block
            ftile[i % 4, s, :, (i // 4) * 128 : (i // 4 + 1) * 128] = block
    alive = [live(row * 8 + half * 4 + y) for half in range(2)]

    pl.semaphore_wait(barrier, 19 - jnp.where(here, 1, 0))

    pending = []

    hop_send, hop_recv = take(2), take(2)
    kept = fmask.at[pl.ds(u_own * 2, 2)]
    given = fmask.at[pl.ds((1 - u_own) * 2, 2)]
    across = rem(x + 2, 4)
    gift = remote(
        given, fg.at[across, to_place, to_yh], hop_send + 1, hop_recv + to_yh,
        at(x_=across, y_=to_y, zh_=to_zh, zl_=to_place),
    )
    gift.start()
    pending.append(gift)
    there = fg.at[x, to_place, to_yh]
    local_kept = pltpu.make_async_copy(kept, there, sems.at[hop_recv + to_yh])
    remote_kept = remote(
        kept, there, hop_send, hop_recv + to_yh, at(y_=to_y, zh_=to_zh, zl_=to_place)
    )

    @pl.when(here)
    def _():
        local_kept.start()

    @pl.when(jnp.logical_not(here))
    def _():
        remote_kept.start()

    pending.append((jnp.logical_not(here), remote_kept))

    a_sems = take(2)
    a_swap = remote(a_ref, abuf.at[k], a_sems, a_sems + 1, partner)
    a_swap.start()
    pending.append(a_swap)
    a_theirs = remote(a_ref, abuf.at[1 - k], a_sems, a_sems + 1, partner)

    r_iota = lax.broadcasted_iota(jnp.int32, (256, 512), 0)
    c_iota = lax.broadcasted_iota(jnp.int32, (256, 512), 1)
    r_y = rem(div(r_iota, 64), 2) * 2 + div(r_iota, 128)
    r_s, r_w = rem(div(r_iota, 32), 2), rem(r_iota, 32)
    same_w = r_w == rem(c_iota, 32)
    for core in range(2):
        hit = same_w & (r_s == div(c_iota, 256)) & (div(rem(c_iota, 256), 32) == r_y * 2 + core)
        perm[core] = jnp.where(hit, 1.0, 0.0).astype(BF16)
    line_send, line_recv, pass_send = take(2), take(4), take(3)
    right_send, right_recv, left_send, left_recv = take(4), take(4), take(4), take(4)
    zh_at = [div(zl, 2), 1 - div(zl, 2)]
    inner = (zl == 1) | (zl == 2)
    even = rem(zl, 2) == 0
    flip1 = jnp.where(even, zl + 1, zl - 1)
    flip2 = rem(zl + 2, 4)
    flip3 = 3 - zl
    order = [zl, flip1, jnp.where(inner, flip3, flip2), jnp.where(inner, flip2, flip3)]

    def along_line(place, sem, to):
        on = (to >= 0) & (to <= 3)
        block = fg.at[x, place]
        copy = remote(block, block, sem, line_recv + place, at(zl_=jnp.clip(to, 0, 3)))
        pl.when(on)(copy.start)
        pending.append((on, copy))

    def along_x(place):
        block = fg.at[x, place]
        for send, recv, device in (
            (right_send, right_recv, right), (left_send, left_recv, left)
        ):
            copy = remote(block, block, send + place, recv + place, device)
            copy.start()
            pending.append(copy)

    for yh in range(2):
        remote(
            kept, fg.at[x, zl, yh], hop_send, hop_recv + yh, around_x[0]
        ).wait_recv()
    along_line(zl, line_send, zl + 1)
    along_line(zl, line_send + 1, zl - 1)
    along_x(zl)
    def arrive_z(i):
        place = order[i]
        block = fg.at[x, place]
        remote(block, block, line_send, line_recv + place, around_x[0]).wait_recv()
        along_line(place, pass_send + i - 1, jnp.where(place > zl, zl - 1, zl + 1))
        along_x(place)

    fr_own_sem = take()
    fr_mine = pltpu.make_async_copy(ftile.at[y], fr.at[:, t, k], sems.at[fr_own_sem])
    fr_mine.start()
    fr_arrive = []

    def share_rows():
        for o in range(1, 8):
            t_to, t_from = rem(t + o, 8), rem(t + 8 - o, 8)
            send, recv = take(), take()
            copy = remote(ftile.at[rem(t_to, 4)], fr.at[:, t, k], send, recv, chip_t(t_to))
            copy.start()
            pending.append(copy)
            fr_arrive.append(
                remote(ftile.at[y], fr.at[:, t_from, k], send, recv, chip_t(t_from))
            )

    g_left, g_right, g_far = rem(x + 3, 4), rem(x + 1, 4), rem(x + 2, 4)
    far_right_send, far_right_recv = take(4), take(4)
    far_left_send, far_left_recv = take(4), take(4)

    def neighbours(i):
        place = order[i]
        for sems_at, group, half, onward, device, back in (
            ((right_send, right_recv), g_left, 0, (far_right_send, far_right_recv), right, left),
            ((left_send, left_recv), g_right, 1, (far_left_send, far_left_recv), left, right),
        ):
            block = fg.at[group, place]
            remote(block, block, sems_at[0] + place, sems_at[1] + place, back).wait_recv()
            part = fg.at[group, place, half]
            copy = remote(part, part, onward[0] + place, onward[1] + place, device)
            copy.start()
            pending.append(copy)

    def far(i):
        place = order[i]
        part = fg.at[g_far, place, 0]
        remote(part, part, far_right_send, far_right_recv + place, left).wait_recv()
        part = fg.at[g_far, place, 1]
        remote(part, part, far_left_send, far_left_recv + place, right).wait_recv()

    u_of = [u_own, 1 - u_own]
    b_of = [rem(place, 2) for place in order]

    def partial(i, w):
        u, place, c = u_of[w], order[i], i * 2 + w

        def body(n, carry):
            rows = pl.ds(pl.multiple_of(n * 256, 256), 256)
            acc = lax.dot_general(
                abuf[0, rows], fg[2 * u, place].reshape(128, 1024), NT_DIMS,
                preferred_element_type=F32,
            )
            acc += lax.dot_general(
                abuf[1, rows], fg[2 * u + 1, place].reshape(128, 1024), NT_DIMS,
                preferred_element_type=F32,
            )
            first = rem(n, 2) * 2
            for j in range(2):
                pp[c, div(n, 2), first + j] = acc[j * 128 : (j + 1) * 128].astype(BF16)
            return carry

        lax.fori_loop(0, 4, body, 0)
        for o in (2, 1, 3):
            sem = y_sems + (c * 3 + o - 1) * 2
            copy = remote(
                pp.at[c, :, rem(y + o, 4)], pyr.at[c, o - 1], sem, sem + 1, around_y[o - 1]
            )
            copy.start()
            pending.append(copy)

    y_sems = take(48)
    z_sems, c_sems = take(8), take(8)
    dy_send, dy_recv = take(8), take(8)
    dx_sems = take(12)
    dz_send, dz_recv = take(8), take(8)

    lane = lax.broadcasted_iota(jnp.int32, (1, 128), 1)
    lane_s = rem(div(lane, 32), 2)
    low = jnp.broadcast_to(lane, (512, 128)) < 64
    lane_live = []
    for w in range(2):
        for half in range(2):
            mask = jnp.zeros((1, 128), F32)
            for s in range(4):
                mask = jnp.where(lane_s + 2 * u_of[w] == s, alive[half][s : s + 1, :], mask)
            lane_live.append(mask)

    def reduce_y(i, w):
        c, step = i * 2 + w, w * 2 + i // 2
        for o in (1, 3, 2):
            sem = y_sems + (c * 3 + o - 1) * 2
            came = around_y[3 - o]
            remote(pp.at[c, :, y], pyr.at[c, o - 1], sem, sem + 1, came).wait_recv()
        sums = []
        for half in range(2):
            acc = pp[c, half, y].astype(F32)
            for o in range(3):
                acc += pyr[c, o, half].astype(F32)
            acc = jnp.where(lane_live[w * 2 + half] > 0, acc, 0.0)
            for s in range(2):
                sb[i, u_of[w], s, half * 128 : (half + 1) * 128] = jnp.where(
                    lane_s == s, acc, 0.0
                ).astype(BF16)
            sums.append(acc)
        lanes = pl.ds(pl.multiple_of(b_of[i] * 128, 128), 128)
        zown[step, :, lanes] = jnp.where(zh == 0, sums[0], sums[1])
        zs[step, :, lanes] = jnp.where(zh == 0, sums[1], sums[0]).astype(BF16)

    def exchange(step):
        copy = remote(
            zs.at[step], zr.at[step], z_sems + step * 2, z_sems + step * 2 + 1, at(zh_=1 - zh)
        )
        copy.start()
        pending.append(copy)
        return copy

    def finish(step, z_copy):
        z_copy.wait_recv()
        pb[step] = (-(zown[step] + zr[step].astype(F32))).astype(BF16)
        theirs = pb.at[step, pl.ds(pl.multiple_of((1 - k) * 64, 64), 64)]
        copy = remote(theirs, cr.at[step], c_sems + step * 2, c_sems + step * 2 + 1, partner)
        copy.start()
        pending.append(copy)
        return copy

    def write_panel(step, c_copy):
        c_copy.wait_recv()
        mine = pb[step, pl.ds(pl.multiple_of(k * 64, 64), 64)]
        res = jnp.dot(mine, perm[k], preferred_element_type=F32)
        res += jnp.dot(cr[step], perm[1 - k], preferred_element_type=F32)
        for s in range(2):
            at_lane = (2 * u_of[step // 2] + s) * 512 + zh_at[step % 2] * 256
            panel_ref[:, pl.ds(pl.multiple_of(at_lane, 256), 256)] = res[
                :, s * 256 : (s + 1) * 256
            ].astype(BF16)

    def products(i):
        both = []
        for u in range(2):
            acc = jnp.zeros((512, 128), F32)
            for s in range(2):
                acc += jnp.dot(
                    fr[2 * u + s].reshape(512, 256), sb[i, u, s], preferred_element_type=F32
                )
            both.append(acc)
        turned = [pltpu.roll(acc, 64, 1) for acc in both]
        ds[i, 0] = jnp.where(low, both[0], turned[1]).astype(BF16)
        ds[i, 1] = jnp.where(low, turned[0], both[1]).astype(BF16)
        half = zh_at[i // 2]
        for yh in range(2):
            y_to = yh * 2 + b_of[i]
            send = remote(
                ds.at[i, yh], dyr.at[half, y], dy_send + i * 2 + yh, dy_recv + half * 4 + y,
                at(y_=y_to),
            )
            pl.when(y_to != y)(send.start)
            pending.append((y_to != y, send))

            @pl.when(y_to == y)
            def _():
                dyr[half, y] = ds[i, yh]

    def over_y(j):
        half = zh_at[j]
        for o in (1, 3, 2):
            y_from = rem(y + o, 4)
            remote(
                ds.at[0, 0], dyr.at[half, y_from], dy_send, dy_recv + half * 4 + y_from,
                around_y[o - 1],
            ).wait_recv()
        for zl_ in range(4):
            rows = slice(zl_ * 128, (zl_ + 1) * 128)
            acc = dyr[half, 0, rows].astype(F32)
            for y_ in range(1, 4):
                acc += dyr[half, y_, rows].astype(F32)
            for x_ in range(4):
                dxs[j, x_, zl_] = acc[x_ * 32 : (x_ + 1) * 32].astype(BF16)
        for o in (2, 1, 3):
            sem = dx_sems + (j * 3 + o - 1) * 2
            copy = remote(
                dxs.at[j, rem(x + o, 4)], dxr.at[j, o - 1], sem, sem + 1, around_x[o - 1]
            )
            copy.start()
            pending.append(copy)

    def over_x(j):
        for o in (1, 3, 2):
            sem = dx_sems + (j * 3 + o - 1) * 2
            remote(
                dxs.at[j, x], dxr.at[j, o - 1], sem, sem + 1, around_x[3 - o]
            ).wait_recv()
        acc = dxs[j, x].astype(F32)
        for o in range(3):
            acc += dxr[j, o].astype(F32)
        dzs[j] = acc.astype(BF16)
        for o in (2, 1, 3, 0):
            zl_to, half = rem(zl + o, 4), zh_at[j]
            mine = half == zh
            copy = remote(
                dzs.at[j, zl_to], dzr.at[z], dz_send + j * 4 + o, dz_recv + z,
                at(zl_=zl_to, zh_=half),
            )
            if o == 0:
                pl.when(jnp.logical_not(mine))(copy.start)
                pending.append((jnp.logical_not(mine), copy))

                @pl.when(mine)
                def _():
                    dzr[z] = dzs[j, zl]

            else:
                copy.start()
                pending.append(copy)

    arrive_z(1)
    neighbours(0)
    loads[4].wait()
    a_theirs.wait_recv()
    partial(0, 0)
    arrive_z(2)
    share_rows()
    neighbours(1)
    partial(1, 0)
    far(0)
    partial(0, 1)
    arrive_z(3)
    neighbours(2)
    reduce_y(0, 0)
    partial(2, 0)
    far(1)
    partial(1, 1)
    reduce_y(1, 0)
    z0 = exchange(0)
    fr_mine.wait()
    for copy in fr_arrive:
        copy.wait_recv()
    fr_sems = take(2)
    fr_swap = remote(fr.at[:, :, k], fr.at[:, :, k], fr_sems, fr_sems + 1, partner)
    fr_swap.start()
    pending.append(fr_swap)
    reduce_y(0, 1)
    neighbours(3)
    partial(3, 0)
    remote(fr.at[:, :, 1 - k], fr.at[:, :, 1 - k], fr_sems, fr_sems + 1, partner).wait_recv()
    products(0)
    far(2)
    partial(2, 1)
    reduce_y(1, 1)
    z2 = exchange(2)
    products(1)
    reduce_y(2, 0)
    far(3)
    partial(3, 1)
    reduce_y(3, 0)
    z1 = exchange(1)
    c0 = finish(0, z0)
    reduce_y(2, 1)
    products(2)
    over_y(0)
    reduce_y(3, 1)
    products(3)
    z3 = exchange(3)
    over_x(0)
    c2 = finish(2, z2)
    c1 = finish(1, z1)
    write_panel(0, c0)
    write_panel(2, c2)
    over_y(1)
    c3 = finish(3, z3)
    write_panel(1, c1)
    over_x(1)
    write_panel(3, c3)
    for o in range(1, 8):
        z_from = rem(z + o, 8)
        remote(dzs.at[0, 0], dzr.at[z_from], dz_send, dz_recv + z_from, chip_z(z_from)).wait_recv()
    total = dzr[0].astype(F32)
    for z_ in range(1, 8):
        total += dzr[z_].astype(F32)
    loads[3].wait()
    for s in range(4):
        diag_ref[s] = inv_ref[s] + total[:, s * 32 : (s + 1) * 32]

    for copy in pending:
        if isinstance(copy, tuple):
            sent, copy = copy
            pl.when(sent)(copy.wait_send)
        else:
            copy.wait_send()
    assert used[0] <= SEMS, used


SEMS = 256


def per_device(inverse_tiles, factor, inverse_diag, tile_list, tile_count):
    vmem = pl.BlockSpec(memory_space=pltpu.VMEM)
    v = pltpu.VMEM
    panel, diag = pl.pallas_call(
        kernel,
        out_shape=(
            jax.ShapeDtypeStruct((64, 2048), BF16),
            jax.ShapeDtypeStruct((4, 32, 32), F32),
        ),
        in_specs=[pl.BlockSpec(memory_space=pl.ANY)] * 5,
        out_specs=(vmem, vmem),
        scratch_shapes=[
            v((4, 128), jnp.int32),
            pltpu.SMEM((4,), jnp.int32),
            v((4, 32, 1024), BF16),
            v((4, 32, 32), F32),
            v((2, 1024, 1024), BF16),
            v((4, 32, 1024), BF16),
            v((4, 4, 32, 256), BF16),
            v((4, 4, 2, 2, 32, 1024), BF16),
            v((4, 8, 2, 32, 256), BF16),
            v((8, 2, 4, 128, 128), BF16),
            v((8, 3, 2, 128, 128), BF16),
            v((4, 2, 2, 256, 128), BF16),
            v((4, 128, 256), F32),
            v((4, 128, 256), BF16),
            v((4, 128, 256), BF16),
            v((4, 128, 256), BF16),
            v((4, 64, 256), BF16),
            v((4, 2, 512, 128), BF16),
            v((2, 4, 512, 128), BF16),
            v((2, 4, 4, 32, 128), BF16),
            v((2, 3, 4, 32, 128), BF16),
            v((2, 4, 32, 128), BF16),
            v((8, 32, 128), BF16),
            v((2, 256, 512), BF16),
            pltpu.SemaphoreType.DMA((SEMS,)),
        ],
        compiler_params=pltpu.CompilerParams(
            collective_id=0, has_side_effects=True, vmem_limit_bytes=60 * 1024 * 1024
        ),
        cost_estimate=pl.CostEstimate(
            flops=2 * 1024 * 2048 * 1024, bytes_accessed=4 << 20, transcendentals=0
        ),
    )(tile_list, tile_count, inverse_tiles, jnp.transpose(factor, (1, 2, 0)), inverse_diag)
    return panel.reshape(64, 4, 512), diag


def solution(mesh):
    return jax.shard_map(
        per_device,
        mesh=mesh,
        in_specs=(P("row", "col"), P("row", None, "col"), P(None, "row", "col"), P(), P()),
        out_specs=(P(("row", "col"), None, None), P(None, "row", "col")),
        check_vma=False,
    )
```

```python
import jax
import jax.numpy as jnp
from jax import lax
from jax.experimental import pallas as pl
from jax.experimental.pallas import tpu as pltpu
from jax.sharding import PartitionSpec as P

MESH = pl.DeviceIdType.MESH
F32 = jnp.float32
BF16 = jnp.bfloat16
NT_DIMS = (((1,), (1,)), ((), ()))


def div(a, b):
    return lax.div(a, jnp.int32(b))


def rem(a, b):
    return lax.rem(a, jnp.int32(b))


def kernel(
    list_hbm, count_hbm, a_ref, ft_hbm, inv_hbm, panel_ref, diag_ref,
    list_ref, count_ref, ft_ref, inv_ref,
    abuf, fmask, ftile, fg, fr, pp, pyr, sb, zown, zs, zr, pb, cr, ds, dyr, dxs, dxr, dzs,
    dzr, perm, sems,
):
    row, col = lax.axis_index("row"), lax.axis_index("col")
    zl, x = div(row, 4), rem(row, 4)
    zh, y, k = div(col, 8), rem(div(col, 2), 4), rem(col, 2)
    z, t = zh * 4 + zl, zh * 4 + y

    def at(zl_=zl, x_=x, zh_=zh, y_=y, k_=k):
        return (zl_ * 4 + x_, zh_ * 8 + y_ * 2 + k_)

    used = [0]

    def take(n=1):
        used[0] += n
        return used[0] - n

    def remote(src, dst, send, recv, device):
        return pltpu.make_async_remote_copy(
            src_ref=src, dst_ref=dst, send_sem=sems.at[send], recv_sem=sems.at[recv],
            device_id=device, device_id_type=MESH,
        )

    partner = at(k_=1 - k)
    around_x = [at(x_=rem(x + o, 4)) for o in (1, 2, 3)]
    around_y = [at(y_=rem(y + o, 4)) for o in (1, 2, 3)]
    right, left = around_x[0], around_x[2]

    def chip_t(t_):
        return at(zh_=div(t_, 4), y_=rem(t_, 4))

    def chip_z(z_, x_=x):
        return at(zh_=div(z_, 4), zl_=rem(z_, 4), x_=x_)

    u_own = div(x, 2)
    to_zh, to_y = div(zl, 2), rem(zl, 2) * 2 + div(x, 2)
    to_place = jnp.where(zh == to_zh, 1 + rem(y, 2), 3 * rem(y, 2))
    to_yh = div(y, 2)
    here = (to_zh == zh) & (to_y == y) & (to_place == zl)

    def half_of(place):
        return jnp.where((place == 1) | (place == 2), zh, 1 - zh)

    def source(yh):
        return at(
            x_=jnp.where(u_own == rem(y, 2), x, rem(x + 2, 4)), y_=yh * 2 + div(zl, 2),
            zh_=half_of(zl), zl_=zh * 2 + div(y, 2),
        )

    first = take(5)
    loads = [
        pltpu.make_async_copy(src, dst, sems.at[first + i])
        for i, (src, dst) in enumerate(
            ((ft_hbm, ft_ref), (list_hbm, list_ref), (count_hbm, count_ref), (inv_hbm, inv_ref),
             (a_ref, abuf.at[k]))
        )
    ]
    for copy in loads:
        copy.start()

    barrier = pltpu.get_barrier_semaphore()

    def greet(device):
        pl.semaphore_signal(barrier, inc=1, device_id=device, device_id_type=MESH)

    greet(partner)
    for device in around_x:
        greet(device)
    for o in range(1, 8):
        greet(chip_t(rem(t + o, 8)))
    for o in range(1, 8):
        if o != 4:
            greet(chip_z(rem(z + o, 8)))

    for yh in range(2):
        s_row, s_col = source(yh)

        @pl.when((s_row != row) | (s_col != col))
        def _():
            greet((s_row, s_col))

    for copy in loads[:3]:
        copy.wait()

    s_iota = lax.broadcasted_iota(jnp.int32, (4, 128), 0)
    p_iota = lax.broadcasted_iota(jnp.int32, (4, 128), 1)
    counts = jnp.zeros((4, 128), jnp.int32)
    for s in range(4):
        counts = jnp.where(s_iota == s, count_ref[s], counts)
    listed = jnp.where(p_iota < counts, list_ref[...], -1)

    def live(tile):
        return jnp.max(jnp.where(listed == tile, 1.0, 0.0), axis=1, keepdims=True)

    for i in range(8):
        alive = live(row * 8 + i)
        for s in range(4):
            block = ft_ref[s, :, i * 128 : (i + 1) * 128]
            keep = jnp.broadcast_to(alive[s : s + 1, :], block.shape) > 0
            block = jnp.where(keep, block.astype(F32), 0.0).astype(BF16)
            fmask[s, :, i * 128 : (i + 1) * 128] = block
            ftile[i % 4, s, :, (i // 4) * 128 : (i // 4 + 1) * 128] = block
    alive = [live(row * 8 + half * 4 + y) for half in range(2)]

    pl.semaphore_wait(barrier, 19 - jnp.where(here, 1, 0))

    pending = []

    hop_send, hop_recv = take(2), take(2)
    kept = fmask.at[pl.ds(u_own * 2, 2)]
    given = fmask.at[pl.ds((1 - u_own) * 2, 2)]
    across = rem(x + 2, 4)
    gift = remote(
        given, fg.at[across, to_place, to_yh], hop_send + 1, hop_recv + to_yh,
        at(x_=across, y_=to_y, zh_=to_zh, zl_=to_place),
    )
    gift.start()
    pending.append(gift)
    there = fg.at[x, to_place, to_yh]
    local_kept = pltpu.make_async_copy(kept, there, sems.at[hop_recv + to_yh])
    remote_kept = remote(
        kept, there, hop_send, hop_recv + to_yh, at(y_=to_y, zh_=to_zh, zl_=to_place)
    )

    @pl.when(here)
    def _():
        local_kept.start()

    @pl.when(jnp.logical_not(here))
    def _():
        remote_kept.start()

    pending.append((jnp.logical_not(here), remote_kept))

    a_sems = take(2)
    a_swap = remote(a_ref, abuf.at[k], a_sems, a_sems + 1, partner)
    a_swap.start()
    pending.append(a_swap)
    a_theirs = remote(a_ref, abuf.at[1 - k], a_sems, a_sems + 1, partner)

    r_iota = lax.broadcasted_iota(jnp.int32, (256, 512), 0)
    c_iota = lax.broadcasted_iota(jnp.int32, (256, 512), 1)
    r_y = rem(div(r_iota, 64), 2) * 2 + div(r_iota, 128)
    r_s, r_w = rem(div(r_iota, 32), 2), rem(r_iota, 32)
    same_w = r_w == rem(c_iota, 32)
    for core in range(2):
        hit = same_w & (r_s == div(c_iota, 256)) & (div(rem(c_iota, 256), 32) == r_y * 2 + core)
        perm[core] = jnp.where(hit, 1.0, 0.0).astype(BF16)
    line_send, line_recv, pass_send = take(2), take(4), take(3)
    right_send, right_recv, left_send, left_recv = take(4), take(4), take(4), take(4)
    zh_at = [zh, 1 - zh]
    inner = (zl == 1) | (zl == 2)
    even = rem(zl, 2) == 0
    flip1 = jnp.where(even, zl + 1, zl - 1)
    flip2 = rem(zl + 2, 4)
    flip3 = 3 - zl
    order = [
        zl, jnp.where(inner, flip3, flip1), jnp.where(inner, flip1, flip2),
        jnp.where(inner, flip2, flip3),
    ]

    def along_line(place, sem, to):
        on = (to >= 0) & (to <= 3)
        block = fg.at[x, place]
        copy = remote(block, block, sem, line_recv + place, at(zl_=jnp.clip(to, 0, 3)))
        pl.when(on)(copy.start)
        pending.append((on, copy))

    def along_x(place):
        block = fg.at[x, place]
        for send, recv, device in (
            (right_send, right_recv, right), (left_send, left_recv, left)
        ):
            copy = remote(block, block, send + place, recv + place, device)
            copy.start()
            pending.append(copy)

    for yh in range(2):
        remote(
            kept, fg.at[x, zl, yh], hop_send, hop_recv + yh, around_x[0]
        ).wait_recv()
    along_line(zl, line_send, zl + 1)
    along_line(zl, line_send + 1, zl - 1)
    along_x(zl)
    def arrive_z(i):
        place = order[i]
        block = fg.at[x, place]
        remote(block, block, line_send, line_recv + place, around_x[0]).wait_recv()
        along_line(place, pass_send + i - 1, jnp.where(place > zl, zl - 1, zl + 1))
        along_x(place)

    fr_own_sem = take()
    fr_mine = pltpu.make_async_copy(ftile.at[y], fr.at[:, t, k], sems.at[fr_own_sem])
    fr_mine.start()
    fr_arrive = []

    def share_rows():
        for o in range(1, 8):
            t_to, t_from = rem(t + o, 8), rem(t + 8 - o, 8)
            send, recv = take(), take()
            copy = remote(ftile.at[rem(t_to, 4)], fr.at[:, t, k], send, recv, chip_t(t_to))
            copy.start()
            pending.append(copy)
            fr_arrive.append(
                remote(ftile.at[y], fr.at[:, t_from, k], send, recv, chip_t(t_from))
            )

    g_left, g_right, g_far = rem(x + 3, 4), rem(x + 1, 4), rem(x + 2, 4)
    far_right_send, far_right_recv = take(4), take(4)
    far_left_send, far_left_recv = take(4), take(4)

    def neighbours(i):
        place = order[i]
        for sems_at, group, half, onward, device, back in (
            ((right_send, right_recv), g_left, 0, (far_right_send, far_right_recv), right, left),
            ((left_send, left_recv), g_right, 1, (far_left_send, far_left_recv), left, right),
        ):
            block = fg.at[group, place]
            remote(block, block, sems_at[0] + place, sems_at[1] + place, back).wait_recv()
            part = fg.at[group, place, half]
            copy = remote(part, part, onward[0] + place, onward[1] + place, device)
            copy.start()
            pending.append(copy)

    def far(i):
        place = order[i]
        part = fg.at[g_far, place, 0]
        remote(part, part, far_right_send, far_right_recv + place, left).wait_recv()
        part = fg.at[g_far, place, 1]
        remote(part, part, far_left_send, far_left_recv + place, right).wait_recv()

    u_of = [u_own, 1 - u_own]
    b_of = [div(place, 2) for place in order]
    half_at = [half_of(place) for place in order]

    def partial(i, w):
        u, place, c = u_of[w], order[i], i * 2 + w

        def body(n, carry):
            rows = pl.ds(pl.multiple_of(n * 256, 256), 256)
            acc = lax.dot_general(
                abuf[0, rows], fg[2 * u, place].reshape(128, 1024), NT_DIMS,
                preferred_element_type=F32,
            )
            acc += lax.dot_general(
                abuf[1, rows], fg[2 * u + 1, place].reshape(128, 1024), NT_DIMS,
                preferred_element_type=F32,
            )
            first = rem(n, 2) * 2
            for j in range(2):
                pp[c, div(n, 2), first + j] = acc[j * 128 : (j + 1) * 128].astype(BF16)
            return carry

        lax.fori_loop(0, 4, body, 0)
        for o in (2, 1, 3):
            sem = y_sems + (c * 3 + o - 1) * 2
            copy = remote(
                pp.at[c, :, rem(y + o, 4)], pyr.at[c, o - 1], sem, sem + 1, around_y[o - 1]
            )
            copy.start()
            pending.append(copy)

    y_sems = take(48)
    z_sems, c_sems = take(8), take(8)
    dy_send, dy_recv = take(8), take(8)
    dx_sems = take(12)
    dz_send, dz_recv = take(8), take(8)

    lane = lax.broadcasted_iota(jnp.int32, (1, 128), 1)
    lane_s = rem(div(lane, 32), 2)
    low = jnp.broadcast_to(lane, (512, 128)) < 64
    lane_live = []
    for w in range(2):
        for half in range(2):
            mask = jnp.zeros((1, 128), F32)
            for s in range(4):
                mask = jnp.where(lane_s + 2 * u_of[w] == s, alive[half][s : s + 1, :], mask)
            lane_live.append(mask)

    def reduce_y(i, w):
        c = i * 2 + w
        step = w * 2 + jnp.where(half_at[i] == zh, 0, 1)
        for o in (1, 3, 2):
            sem = y_sems + (c * 3 + o - 1) * 2
            came = around_y[3 - o]
            remote(pp.at[c, :, y], pyr.at[c, o - 1], sem, sem + 1, came).wait_recv()
        sums = []
        for half in range(2):
            acc = pp[c, half, y].astype(F32)
            for o in range(3):
                acc += pyr[c, o, half].astype(F32)
            acc = jnp.where(lane_live[w * 2 + half] > 0, acc, 0.0)
            for s in range(2):
                sb[i, u_of[w], s, half * 128 : (half + 1) * 128] = jnp.where(
                    lane_s == s, acc, 0.0
                ).astype(BF16)
            sums.append(acc)
        lanes = pl.ds(pl.multiple_of(b_of[i] * 128, 128), 128)
        zown[step, :, lanes] = jnp.where(zh == 0, sums[0], sums[1])
        zs[step, :, lanes] = jnp.where(zh == 0, sums[1], sums[0]).astype(BF16)

    def exchange(step):
        other = step + 1 - 2 * (step % 2)
        device = at(zh_=1 - zh)
        copy = remote(
            zs.at[step], zr.at[other], z_sems + step * 2, z_sems + other * 2 + 1, device
        )
        copy.start()
        pending.append(copy)
        return remote(
            zs.at[other], zr.at[step], z_sems + other * 2, z_sems + step * 2 + 1, device
        )

    def finish(step, z_copy):
        z_copy.wait_recv()
        pb[step] = (-(zown[step] + zr[step].astype(F32))).astype(BF16)
        theirs = pb.at[step, pl.ds(pl.multiple_of((1 - k) * 64, 64), 64)]
        copy = remote(theirs, cr.at[step], c_sems + step * 2, c_sems + step * 2 + 1, partner)
        copy.start()
        pending.append(copy)
        return copy

    def write_panel(step, c_copy):
        c_copy.wait_recv()
        mine = pb[step, pl.ds(pl.multiple_of(k * 64, 64), 64)]
        res = jnp.dot(mine, perm[k], preferred_element_type=F32)
        res += jnp.dot(cr[step], perm[1 - k], preferred_element_type=F32)
        for s in range(2):
            at_lane = (2 * u_of[step // 2] + s) * 512 + zh_at[step % 2] * 256
            panel_ref[:, pl.ds(pl.multiple_of(at_lane, 256), 256)] = res[
                :, s * 256 : (s + 1) * 256
            ].astype(BF16)

    def products(i):
        both = []
        for u in range(2):
            acc = jnp.zeros((512, 128), F32)
            for s in range(2):
                acc += jnp.dot(
                    fr[2 * u + s].reshape(512, 256), sb[i, u, s], preferred_element_type=F32
                )
            both.append(acc)
        turned = [pltpu.roll(acc, 64, 1) for acc in both]
        ds[i, 0] = jnp.where(low, both[0], turned[1]).astype(BF16)
        ds[i, 1] = jnp.where(low, turned[0], both[1]).astype(BF16)
        half = half_at[i]
        for yh in range(2):
            y_to = yh * 2 + b_of[i]
            send = remote(
                ds.at[i, yh], dyr.at[half, y], dy_send + i * 2 + yh, dy_recv + half * 4 + y,
                at(y_=y_to),
            )
            pl.when(y_to != y)(send.start)
            pending.append((y_to != y, send))

            @pl.when(y_to == y)
            def _():
                dyr[half, y] = ds[i, yh]

    def over_y(j):
        half = zh_at[j]
        for o in (1, 3, 2):
            y_from = rem(y + o, 4)
            remote(
                ds.at[0, 0], dyr.at[half, y_from], dy_send, dy_recv + half * 4 + y_from,
                around_y[o - 1],
            ).wait_recv()
        for zl_ in range(4):
            rows = slice(zl_ * 128, (zl_ + 1) * 128)
            acc = dyr[half, 0, rows].astype(F32)
            for y_ in range(1, 4):
                acc += dyr[half, y_, rows].astype(F32)
            for x_ in range(4):
                dxs[j, x_, zl_] = acc[x_ * 32 : (x_ + 1) * 32].astype(BF16)
        for o in (2, 1, 3):
            sem = dx_sems + (j * 3 + o - 1) * 2
            copy = remote(
                dxs.at[j, rem(x + o, 4)], dxr.at[j, o - 1], sem, sem + 1, around_x[o - 1]
            )
            copy.start()
            pending.append(copy)

    def over_x(j):
        for o in (1, 3, 2):
            sem = dx_sems + (j * 3 + o - 1) * 2
            remote(
                dxs.at[j, x], dxr.at[j, o - 1], sem, sem + 1, around_x[3 - o]
            ).wait_recv()
        acc = dxs[j, x].astype(F32)
        for o in range(3):
            acc += dxr[j, o].astype(F32)
        dzs[j] = acc.astype(BF16)
        for o in (2, 1, 3, 0):
            zl_to, half = rem(zl + o, 4), zh_at[j]
            if half is zh and o == 0:
                dzr[z] = dzs[j, zl]
                continue
            copy = remote(
                dzs.at[j, zl_to], dzr.at[z], dz_send + j * 4 + o, dz_recv + z,
                at(zl_=zl_to, zh_=half),
            )
            copy.start()
            pending.append(copy)

    arrive_z(1)
    neighbours(0)
    loads[4].wait()
    a_theirs.wait_recv()
    partial(0, 0)
    arrive_z(2)
    neighbours(1)
    partial(1, 0)
    far(0)
    partial(0, 1)
    arrive_z(3)
    neighbours(2)
    share_rows()
    reduce_y(0, 0)
    partial(2, 0)
    far(1)
    partial(1, 1)
    reduce_y(1, 0)
    reduce_y(0, 1)
    neighbours(3)
    partial(3, 0)
    reduce_y(2, 0)
    z0 = exchange(0)
    fr_mine.wait()
    for copy in fr_arrive:
        copy.wait_recv()
    fr_sems = take(2)
    fr_swap = remote(fr.at[:, :, k], fr.at[:, :, k], fr_sems, fr_sems + 1, partner)
    fr_swap.start()
    pending.append(fr_swap)
    reduce_y(1, 1)
    far(2)
    partial(2, 1)
    remote(fr.at[:, :, 1 - k], fr.at[:, :, 1 - k], fr_sems, fr_sems + 1, partner).wait_recv()
    products(0)
    products(1)
    far(3)
    partial(3, 1)
    reduce_y(2, 1)
    products(2)
    over_y(0)
    reduce_y(3, 0)
    reduce_y(3, 1)
    products(3)
    z2 = exchange(2)
    z1 = exchange(1)
    z3 = exchange(3)
    over_x(0)
    c0 = finish(0, z0)
    c2 = finish(2, z2)
    c1 = finish(1, z1)
    write_panel(0, c0)
    write_panel(2, c2)
    over_y(1)
    c3 = finish(3, z3)
    write_panel(1, c1)
    over_x(1)
    write_panel(3, c3)
    for o in range(1, 8):
        z_from = rem(z + o, 8)
        remote(dzs.at[0, 0], dzr.at[z_from], dz_send, dz_recv + z_from, chip_z(z_from)).wait_recv()
    total = dzr[0].astype(F32)
    for z_ in range(1, 8):
        total += dzr[z_].astype(F32)
    loads[3].wait()
    for s in range(4):
        diag_ref[s] = inv_ref[s] + total[:, s * 32 : (s + 1) * 32]

    for copy in pending:
        if isinstance(copy, tuple):
            sent, copy = copy
            pl.when(sent)(copy.wait_send)
        else:
            copy.wait_send()
    assert used[0] <= SEMS, used


SEMS = 256


def per_device(inverse_tiles, factor, inverse_diag, tile_list, tile_count):
    vmem = pl.BlockSpec(memory_space=pltpu.VMEM)
    v = pltpu.VMEM
    panel, diag = pl.pallas_call(
        kernel,
        out_shape=(
            jax.ShapeDtypeStruct((64, 2048), BF16),
            jax.ShapeDtypeStruct((4, 32, 32), F32),
        ),
        in_specs=[pl.BlockSpec(memory_space=pl.ANY)] * 5,
        out_specs=(vmem, vmem),
        scratch_shapes=[
            v((4, 128), jnp.int32),
            pltpu.SMEM((4,), jnp.int32),
            v((4, 32, 1024), BF16),
            v((4, 32, 32), F32),
            v((2, 1024, 1024), BF16),
            v((4, 32, 1024), BF16),
            v((4, 4, 32, 256), BF16),
            v((4, 4, 2, 2, 32, 1024), BF16),
            v((4, 8, 2, 32, 256), BF16),
            v((8, 2, 4, 128, 128), BF16),
            v((8, 3, 2, 128, 128), BF16),
            v((4, 2, 2, 256, 128), BF16),
            v((4, 128, 256), F32),
            v((4, 128, 256), BF16),
            v((4, 128, 256), BF16),
            v((4, 128, 256), BF16),
            v((4, 64, 256), BF16),
            v((4, 2, 512, 128), BF16),
            v((2, 4, 512, 128), BF16),
            v((2, 4, 4, 32, 128), BF16),
            v((2, 3, 4, 32, 128), BF16),
            v((2, 4, 32, 128), BF16),
            v((8, 32, 128), BF16),
            v((2, 256, 512), BF16),
            pltpu.SemaphoreType.DMA((SEMS,)),
        ],
        compiler_params=pltpu.CompilerParams(
            collective_id=0, has_side_effects=True, vmem_limit_bytes=60 * 1024 * 1024
        ),
        cost_estimate=pl.CostEstimate(
            flops=2 * 1024 * 2048 * 1024, bytes_accessed=4 << 20, transcendentals=0
        ),
    )(tile_list, tile_count, inverse_tiles, jnp.transpose(factor, (1, 2, 0)), inverse_diag)
    return panel.reshape(64, 4, 512), diag


def solution(mesh):
    return jax.shard_map(
        per_device,
        mesh=mesh,
        in_specs=(P("row", "col"), P("row", None, "col"), P(None, "row", "col"), P(), P()),
        out_specs=(P(("row", "col"), None, None), P(None, "row", "col")),
        check_vma=False,
    )
```

```python
import jax
import jax.numpy as jnp
from jax import lax
from jax.experimental import pallas as pl
from jax.experimental.pallas import tpu as pltpu
from jax.sharding import PartitionSpec as P

MESH = pl.DeviceIdType.MESH
F32 = jnp.float32
BF16 = jnp.bfloat16
NT_DIMS = (((1,), (1,)), ((), ()))


def div(a, b):
    return lax.div(a, jnp.int32(b))


def rem(a, b):
    return lax.rem(a, jnp.int32(b))


def kernel(
    list_hbm, count_hbm, a_ref, ft_hbm, inv_hbm, panel_ref, diag_ref,
    list_ref, count_ref, ft_ref, inv_ref,
    abuf, fmask, ftile, fg, fr, pp, pyr, sb, zown, zs, zr, pb, cr, dxs, dxr, dys, dyr, dzs,
    dzr, perm, sems,
):
    row, col = lax.axis_index("row"), lax.axis_index("col")
    zl, x = div(row, 4), rem(row, 4)
    zh, y, k = div(col, 8), rem(div(col, 2), 4), rem(col, 2)
    z, t = zh * 4 + zl, zh * 4 + y

    def at(zl_=zl, x_=x, zh_=zh, y_=y, k_=k):
        return (zl_ * 4 + x_, zh_ * 8 + y_ * 2 + k_)

    used = [0]

    def take(n=1):
        used[0] += n
        return used[0] - n

    def remote(src, dst, send, recv, device):
        return pltpu.make_async_remote_copy(
            src_ref=src, dst_ref=dst, send_sem=sems.at[send], recv_sem=sems.at[recv],
            device_id=device, device_id_type=MESH,
        )

    partner = at(k_=1 - k)
    around_x = [at(x_=rem(x + o, 4)) for o in (1, 2, 3)]
    around_y = [at(y_=rem(y + o, 4)) for o in (1, 2, 3)]
    right, left = around_x[0], around_x[2]

    def chip_t(t_):
        return at(zh_=div(t_, 4), y_=rem(t_, 4))

    def chip_z(z_, x_=x):
        return at(zh_=div(z_, 4), zl_=rem(z_, 4), x_=x_)

    u_own = div(x, 2)
    to_zh, to_y = div(zl, 2), rem(zl, 2) * 2 + div(x, 2)
    to_place = jnp.where(zh == to_zh, 1 + rem(y, 2), 3 * rem(y, 2))
    to_yh = div(y, 2)
    here = (to_zh == zh) & (to_y == y) & (to_place == zl)

    def half_of(place):
        return jnp.where((place == 1) | (place == 2), zh, 1 - zh)

    def source(yh):
        return at(
            x_=jnp.where(u_own == rem(y, 2), x, rem(x + 2, 4)), y_=yh * 2 + div(zl, 2),
            zh_=half_of(zl), zl_=zh * 2 + div(y, 2),
        )

    first = take(5)
    loads = [
        pltpu.make_async_copy(src, dst, sems.at[first + i])
        for i, (src, dst) in enumerate(
            ((ft_hbm, ft_ref), (list_hbm, list_ref), (count_hbm, count_ref), (inv_hbm, inv_ref),
             (a_ref, abuf.at[k]))
        )
    ]
    for copy in loads:
        copy.start()

    barrier = pltpu.get_barrier_semaphore()

    def greet(device):
        pl.semaphore_signal(barrier, inc=1, device_id=device, device_id_type=MESH)

    greet(partner)
    for device in around_x:
        greet(device)
    for o in range(1, 8):
        greet(chip_t(rem(t + o, 8)))
    for o in range(1, 8):
        if o != 4:
            greet(chip_z(rem(z + o, 8)))

    for yh in range(2):
        s_row, s_col = source(yh)

        @pl.when((s_row != row) | (s_col != col))
        def _():
            greet((s_row, s_col))

    for copy in loads[:3]:
        copy.wait()

    s_iota = lax.broadcasted_iota(jnp.int32, (4, 128), 0)
    p_iota = lax.broadcasted_iota(jnp.int32, (4, 128), 1)
    counts = jnp.zeros((4, 128), jnp.int32)
    for s in range(4):
        counts = jnp.where(s_iota == s, count_ref[s], counts)
    listed = jnp.where(p_iota < counts, list_ref[...], -1)

    def live(tile):
        return jnp.max(jnp.where(listed == tile, 1.0, 0.0), axis=1, keepdims=True)

    for i in range(8):
        alive = live(row * 8 + i)
        for s in range(4):
            block = ft_ref[s, :, i * 128 : (i + 1) * 128]
            keep = jnp.broadcast_to(alive[s : s + 1, :], block.shape) > 0
            block = jnp.where(keep, block.astype(F32), 0.0).astype(BF16)
            fmask[s, :, i * 128 : (i + 1) * 128] = block
            ftile[i % 4, s, :, (i // 4) * 128 : (i // 4 + 1) * 128] = block
    alive = [live(row * 8 + half * 4 + y) for half in range(2)]

    pl.semaphore_wait(barrier, 19 - jnp.where(here, 1, 0))

    pending = []

    hop_send, hop_recv = take(2), take(2)
    kept = fmask.at[pl.ds(u_own * 2, 2)]
    given = fmask.at[pl.ds((1 - u_own) * 2, 2)]
    across = rem(x + 2, 4)
    gift = remote(
        given, fg.at[across, to_place, to_yh], hop_send + 1, hop_recv + to_yh,
        at(x_=across, y_=to_y, zh_=to_zh, zl_=to_place),
    )
    gift.start()
    pending.append(gift)
    there = fg.at[x, to_place, to_yh]
    local_kept = pltpu.make_async_copy(kept, there, sems.at[hop_recv + to_yh])
    remote_kept = remote(
        kept, there, hop_send, hop_recv + to_yh, at(y_=to_y, zh_=to_zh, zl_=to_place)
    )

    @pl.when(here)
    def _():
        local_kept.start()

    @pl.when(jnp.logical_not(here))
    def _():
        remote_kept.start()

    pending.append((jnp.logical_not(here), remote_kept))

    a_sems = take(2)
    a_swap = remote(a_ref, abuf.at[k], a_sems, a_sems + 1, partner)
    a_swap.start()
    pending.append(a_swap)
    a_theirs = remote(a_ref, abuf.at[1 - k], a_sems, a_sems + 1, partner)

    r_iota = lax.broadcasted_iota(jnp.int32, (256, 512), 0)
    c_iota = lax.broadcasted_iota(jnp.int32, (256, 512), 1)
    r_y = rem(div(r_iota, 64), 2) * 2 + div(r_iota, 128)
    r_s, r_w = rem(div(r_iota, 32), 2), rem(r_iota, 32)
    same_w = r_w == rem(c_iota, 32)
    for core in range(2):
        hit = same_w & (r_s == div(c_iota, 256)) & (div(rem(c_iota, 256), 32) == r_y * 2 + core)
        perm[core] = jnp.where(hit, 1.0, 0.0).astype(BF16)
    line_send, line_recv, pass_send = take(2), take(4), take(3)
    right_send, right_recv, left_send, left_recv = take(4), take(4), take(4), take(4)
    zh_at = [zh, 1 - zh]
    inner = (zl == 1) | (zl == 2)
    even = rem(zl, 2) == 0
    flip1 = jnp.where(even, zl + 1, zl - 1)
    flip2 = rem(zl + 2, 4)
    flip3 = 3 - zl
    order = [
        zl, jnp.where(inner, flip3, flip1), jnp.where(inner, flip1, flip2),
        jnp.where(inner, flip2, flip3),
    ]

    def along_line(place, sem, to):
        on = (to >= 0) & (to <= 3)
        block = fg.at[x, place]
        copy = remote(block, block, sem, line_recv + place, at(zl_=jnp.clip(to, 0, 3)))
        pl.when(on)(copy.start)
        pending.append((on, copy))

    def along_x(place):
        block = fg.at[x, place]
        for send, recv, device in (
            (right_send, right_recv, right), (left_send, left_recv, left)
        ):
            copy = remote(block, block, send + place, recv + place, device)
            copy.start()
            pending.append(copy)

    for yh in range(2):
        remote(
            kept, fg.at[x, zl, yh], hop_send, hop_recv + yh, around_x[0]
        ).wait_recv()
    along_line(zl, line_send, zl + 1)
    along_line(zl, line_send + 1, zl - 1)
    along_x(zl)
    def arrive_z(i):
        place = order[i]
        block = fg.at[x, place]
        remote(block, block, line_send, line_recv + place, around_x[0]).wait_recv()
        along_line(place, pass_send + i - 1, jnp.where(place > zl, zl - 1, zl + 1))
        along_x(place)

    fr_own_sem = take()
    fr_mine = pltpu.make_async_copy(ftile.at[y], fr.at[:, t, k], sems.at[fr_own_sem])
    fr_mine.start()
    fr_arrive = []

    def share_rows():
        for o in range(1, 8):
            t_to, t_from = rem(t + o, 8), rem(t + 8 - o, 8)
            send, recv = take(), take()
            copy = remote(ftile.at[rem(t_to, 4)], fr.at[:, t, k], send, recv, chip_t(t_to))
            copy.start()
            pending.append(copy)
            fr_arrive.append(
                remote(ftile.at[y], fr.at[:, t_from, k], send, recv, chip_t(t_from))
            )

    g_left, g_right, g_far = rem(x + 3, 4), rem(x + 1, 4), rem(x + 2, 4)
    far_right_send, far_right_recv = take(4), take(4)
    far_left_send, far_left_recv = take(4), take(4)

    def neighbours(i):
        place = order[i]
        for sems_at, group, half, onward, device, back in (
            ((right_send, right_recv), g_left, 0, (far_right_send, far_right_recv), right, left),
            ((left_send, left_recv), g_right, 1, (far_left_send, far_left_recv), left, right),
        ):
            block = fg.at[group, place]
            remote(block, block, sems_at[0] + place, sems_at[1] + place, back).wait_recv()
            part = fg.at[group, place, half]
            copy = remote(part, part, onward[0] + place, onward[1] + place, device)
            copy.start()
            pending.append(copy)

    def far(i):
        place = order[i]
        part = fg.at[g_far, place, 0]
        remote(part, part, far_right_send, far_right_recv + place, left).wait_recv()
        part = fg.at[g_far, place, 1]
        remote(part, part, far_left_send, far_left_recv + place, right).wait_recv()

    u_of = [u_own, 1 - u_own]
    b_of = [div(place, 2) for place in order]
    half_at = [half_of(place) for place in order]

    def partial(i, w):
        u, place, c = u_of[w], order[i], i * 2 + w

        def body(n, carry):
            rows = pl.ds(pl.multiple_of(n * 256, 256), 256)
            acc = lax.dot_general(
                abuf[0, rows], fg[2 * u, place].reshape(128, 1024), NT_DIMS,
                preferred_element_type=F32,
            )
            acc += lax.dot_general(
                abuf[1, rows], fg[2 * u + 1, place].reshape(128, 1024), NT_DIMS,
                preferred_element_type=F32,
            )
            first = rem(n, 2) * 2
            for j in range(2):
                pp[c, div(n, 2), first + j] = acc[j * 128 : (j + 1) * 128].astype(BF16)
            return carry

        lax.fori_loop(0, 4, body, 0)
        for o in (2, 1, 3):
            sem = y_sems + (c * 3 + o - 1) * 2
            copy = remote(
                pp.at[c, :, rem(y + o, 4)], pyr.at[c, o - 1], sem, sem + 1, around_y[o - 1]
            )
            copy.start()
            pending.append(copy)

    y_sems = take(48)
    z_sems, c_sems = take(8), take(8)
    dy_send, dy_recv = take(8), take(8)
    dx_sems = take(24)
    dz_send, dz_recv = take(8), take(8)

    lane = lax.broadcasted_iota(jnp.int32, (1, 128), 1)
    lane_s = rem(div(lane, 32), 2)
    low = jnp.broadcast_to(lane, (512, 128)) < 64
    lane_live = []
    for w in range(2):
        for half in range(2):
            mask = jnp.zeros((1, 128), F32)
            for s in range(4):
                mask = jnp.where(lane_s + 2 * u_of[w] == s, alive[half][s : s + 1, :], mask)
            lane_live.append(mask)

    def reduce_y(i, w):
        c = i * 2 + w
        step = w * 2 + jnp.where(half_at[i] == zh, 0, 1)
        for o in (1, 3, 2):
            sem = y_sems + (c * 3 + o - 1) * 2
            came = around_y[3 - o]
            remote(pp.at[c, :, y], pyr.at[c, o - 1], sem, sem + 1, came).wait_recv()
        sums = []
        for half in range(2):
            acc = pp[c, half, y].astype(F32)
            for o in range(3):
                acc += pyr[c, o, half].astype(F32)
            acc = jnp.where(lane_live[w * 2 + half] > 0, acc, 0.0)
            for s in range(2):
                sb[i, u_of[w], s, half * 128 : (half + 1) * 128] = jnp.where(
                    lane_s == s, acc, 0.0
                ).astype(BF16)
            sums.append(acc)
        lanes = pl.ds(pl.multiple_of(b_of[i] * 128, 128), 128)
        zown[step, :, lanes] = jnp.where(zh == 0, sums[0], sums[1])
        zs[step, :, lanes] = jnp.where(zh == 0, sums[1], sums[0]).astype(BF16)

    def exchange(step):
        other = step + 1 - 2 * (step % 2)
        device = at(zh_=1 - zh)
        copy = remote(
            zs.at[step], zr.at[other], z_sems + step * 2, z_sems + other * 2 + 1, device
        )
        copy.start()
        pending.append(copy)
        return remote(
            zs.at[other], zr.at[step], z_sems + other * 2, z_sems + step * 2 + 1, device
        )

    def finish(step, z_copy):
        z_copy.wait_recv()
        pb[step] = (-(zown[step] + zr[step].astype(F32))).astype(BF16)
        theirs = pb.at[step, pl.ds(pl.multiple_of((1 - k) * 64, 64), 64)]
        copy = remote(theirs, cr.at[step], c_sems + step * 2, c_sems + step * 2 + 1, partner)
        copy.start()
        pending.append(copy)
        return copy

    def write_panel(step, c_copy):
        c_copy.wait_recv()
        mine = pb[step, pl.ds(pl.multiple_of(k * 64, 64), 64)]
        res = jnp.dot(mine, perm[k], preferred_element_type=F32)
        res += jnp.dot(cr[step], perm[1 - k], preferred_element_type=F32)
        for s in range(2):
            at_lane = (2 * u_of[step // 2] + s) * 512 + zh_at[step % 2] * 256
            panel_ref[:, pl.ds(pl.multiple_of(at_lane, 256), 256)] = res[
                :, s * 256 : (s + 1) * 256
            ].astype(BF16)

    def products(i):
        both = []
        for u in range(2):
            acc = jnp.zeros((512, 128), F32)
            for s in range(2):
                acc += jnp.dot(
                    fr[2 * u + s].reshape(512, 256), sb[i, u, s], preferred_element_type=F32
                )
            both.append(acc)
        turned = [pltpu.roll(acc, 64, 1) for acc in both]
        tiles = (jnp.where(low, both[0], turned[1]), jnp.where(low, turned[0], both[1]))
        for yh in range(2):
            for zl_ in range(4):
                for x_ in range(4):
                    first = zl_ * 128 + x_ * 32
                    dxs[i, x_, yh, zl_] = tiles[yh][first : first + 32].astype(BF16)
        for o in (2, 1, 3):
            sem = dx_sems + (i * 3 + o - 1) * 2
            copy = remote(
                dxs.at[i, rem(x + o, 4)], dxr.at[i, o - 1], sem, sem + 1, around_x[o - 1]
            )
            copy.start()
            pending.append(copy)

    def over_x(i):
        for o in (1, 3, 2):
            sem = dx_sems + (i * 3 + o - 1) * 2
            remote(
                dxs.at[i, x], dxr.at[i, o - 1], sem, sem + 1, around_x[3 - o]
            ).wait_recv()
        acc = dxs[i, x].astype(F32)
        for o in range(3):
            acc += dxr[i, o].astype(F32)
        dys[i] = acc.astype(BF16)
        half = half_at[i]
        for yh in range(2):
            y_to = yh * 2 + b_of[i]
            send = remote(
                dys.at[i, yh], dyr.at[half, y], dy_send + i * 2 + yh, dy_recv + half * 4 + y,
                at(y_=y_to),
            )
            pl.when(y_to != y)(send.start)
            pending.append((y_to != y, send))

            @pl.when(y_to == y)
            def _():
                dyr[half, y] = dys[i, yh]

    def over_y(j):
        half = zh_at[j]
        for o in (1, 3, 2):
            y_from = rem(y + o, 4)
            remote(
                dys.at[0, 0], dyr.at[half, y_from], dy_send, dy_recv + half * 4 + y_from,
                around_y[o - 1],
            ).wait_recv()
        acc = dyr[half, 0].astype(F32)
        for y_ in range(1, 4):
            acc += dyr[half, y_].astype(F32)
        dzs[j] = acc.astype(BF16)
        for o in (2, 1, 3, 0):
            zl_to = rem(zl + o, 4)
            if j == 0 and o == 0:
                dzr[z] = dzs[j, zl]
                continue
            copy = remote(
                dzs.at[j, zl_to], dzr.at[z], dz_send + j * 4 + o, dz_recv + z,
                at(zl_=zl_to, zh_=half),
            )
            copy.start()
            pending.append(copy)

    arrive_z(1)
    neighbours(0)
    loads[4].wait()
    a_theirs.wait_recv()
    partial(0, 0)
    arrive_z(2)
    neighbours(1)
    partial(1, 0)
    far(0)
    partial(0, 1)
    arrive_z(3)
    share_rows()
    neighbours(2)
    reduce_y(0, 0)
    partial(2, 0)
    far(1)
    partial(1, 1)
    reduce_y(1, 0)
    reduce_y(0, 1)
    neighbours(3)
    partial(3, 0)
    reduce_y(2, 0)
    reduce_y(1, 1)
    far(2)
    partial(2, 1)
    z0 = exchange(0)
    fr_mine.wait()
    for copy in fr_arrive:
        copy.wait_recv()
    fr_sems = take(2)
    fr_swap = remote(fr.at[:, :, k], fr.at[:, :, k], fr_sems, fr_sems + 1, partner)
    fr_swap.start()
    pending.append(fr_swap)
    far(3)
    partial(3, 1)
    reduce_y(3, 0)
    z1 = exchange(1)
    reduce_y(2, 1)
    z2 = exchange(2)
    remote(fr.at[:, :, 1 - k], fr.at[:, :, 1 - k], fr_sems, fr_sems + 1, partner).wait_recv()
    products(0)
    products(1)
    reduce_y(3, 1)
    products(2)
    products(3)
    z3 = exchange(3)
    over_x(0)
    over_x(1)
    c0 = finish(0, z0)
    over_x(2)
    c2 = finish(2, z2)
    over_y(0)
    c1 = finish(1, z1)
    over_x(3)
    write_panel(0, c0)
    write_panel(2, c2)
    over_y(1)
    c3 = finish(3, z3)
    write_panel(1, c1)
    write_panel(3, c3)
    for o in range(1, 8):
        z_from = rem(z + o, 8)
        remote(dzs.at[0, 0], dzr.at[z_from], dz_send, dz_recv + z_from, chip_z(z_from)).wait_recv()
    total = dzr[0].astype(F32)
    for z_ in range(1, 8):
        total += dzr[z_].astype(F32)
    loads[3].wait()
    for s in range(4):
        diag_ref[s] = inv_ref[s] + total[:, s * 32 : (s + 1) * 32]

    for copy in pending:
        if isinstance(copy, tuple):
            sent, copy = copy
            pl.when(sent)(copy.wait_send)
        else:
            copy.wait_send()
    assert used[0] <= SEMS, used


SEMS = 264


def per_device(inverse_tiles, factor, inverse_diag, tile_list, tile_count):
    vmem = pl.BlockSpec(memory_space=pltpu.VMEM)
    v = pltpu.VMEM
    panel, diag = pl.pallas_call(
        kernel,
        out_shape=(
            jax.ShapeDtypeStruct((64, 2048), BF16),
            jax.ShapeDtypeStruct((4, 32, 32), F32),
        ),
        in_specs=[pl.BlockSpec(memory_space=pl.ANY)] * 5,
        out_specs=(vmem, vmem),
        scratch_shapes=[
            v((4, 128), jnp.int32),
            pltpu.SMEM((4,), jnp.int32),
            v((4, 32, 1024), BF16),
            v((4, 32, 32), F32),
            v((2, 1024, 1024), BF16),
            v((4, 32, 1024), BF16),
            v((4, 4, 32, 256), BF16),
            v((4, 4, 2, 2, 32, 1024), BF16),
            v((4, 8, 2, 32, 256), BF16),
            v((8, 2, 4, 128, 128), BF16),
            v((8, 3, 2, 128, 128), BF16),
            v((4, 2, 2, 256, 128), BF16),
            v((4, 128, 256), F32),
            v((4, 128, 256), BF16),
            v((4, 128, 256), BF16),
            v((4, 128, 256), BF16),
            v((4, 64, 256), BF16),
            v((4, 4, 2, 4, 32, 128), BF16),
            v((4, 3, 2, 4, 32, 128), BF16),
            v((4, 2, 4, 32, 128), BF16),
            v((2, 4, 4, 32, 128), BF16),
            v((2, 4, 32, 128), BF16),
            v((8, 32, 128), BF16),
            v((2, 256, 512), BF16),
            pltpu.SemaphoreType.DMA((SEMS,)),
        ],
        compiler_params=pltpu.CompilerParams(
            collective_id=0, has_side_effects=True, vmem_limit_bytes=60 * 1024 * 1024
        ),
        cost_estimate=pl.CostEstimate(
            flops=2 * 1024 * 2048 * 1024, bytes_accessed=4 << 20, transcendentals=0
        ),
    )(tile_list, tile_count, inverse_tiles, jnp.transpose(factor, (1, 2, 0)), inverse_diag)
    return panel.reshape(64, 4, 512), diag


def solution(mesh):
    return jax.shard_map(
        per_device,
        mesh=mesh,
        in_specs=(P("row", "col"), P("row", None, "col"), P(None, "row", "col"), P(), P()),
        out_specs=(P(("row", "col"), None, None), P(None, "row", "col")),
        check_vma=False,
    )
```

```python
import jax
import jax.numpy as jnp
from jax import lax
from jax.experimental import pallas as pl
from jax.experimental.pallas import tpu as pltpu
from jax.sharding import PartitionSpec as P

MESH = pl.DeviceIdType.MESH
F32 = jnp.float32
BF16 = jnp.bfloat16
NT_DIMS = (((1,), (1,)), ((), ()))


def div(a, b):
    return lax.div(a, jnp.int32(b))


def rem(a, b):
    return lax.rem(a, jnp.int32(b))


def kernel(
    list_hbm, count_hbm, a_ref, ft_hbm, inv_hbm, panel_ref, diag_ref,
    list_ref, count_ref, ft_ref, inv_ref,
    abuf, fmask, ftile, fg, fr, pp, pyr, sb, zown, zs, zr, pb, cr, dxs, dxr, dys, dyr, dzs,
    dzr, perm, sems,
):
    row, col = lax.axis_index("row"), lax.axis_index("col")
    zl, x = div(row, 4), rem(row, 4)
    zh, y, k = div(col, 8), rem(div(col, 2), 4), rem(col, 2)
    z, t = zh * 4 + zl, zh * 4 + y

    def at(zl_=zl, x_=x, zh_=zh, y_=y, k_=k):
        return (zl_ * 4 + x_, zh_ * 8 + y_ * 2 + k_)

    used = [0]

    def take(n=1):
        used[0] += n
        return used[0] - n

    def remote(src, dst, send, recv, device):
        return pltpu.make_async_remote_copy(
            src_ref=src, dst_ref=dst, send_sem=sems.at[send], recv_sem=sems.at[recv],
            device_id=device, device_id_type=MESH,
        )

    partner = at(k_=1 - k)
    around_x = [at(x_=rem(x + o, 4)) for o in (1, 2, 3)]
    around_y = [at(y_=rem(y + o, 4)) for o in (1, 2, 3)]
    right, left = around_x[0], around_x[2]

    def chip_t(t_):
        return at(zh_=div(t_, 4), y_=rem(t_, 4))

    def chip_z(z_, x_=x):
        return at(zh_=div(z_, 4), zl_=rem(z_, 4), x_=x_)

    u_own = div(x, 2)
    to_zh, to_y = div(zl, 2), rem(zl, 2) * 2 + div(x, 2)
    to_place = jnp.where(zh == to_zh, 1 + rem(y, 2), 3 * rem(y, 2))
    to_yh = div(y, 2)
    here = (to_zh == zh) & (to_y == y) & (to_place == zl)

    def half_of(place):
        return jnp.where((place == 1) | (place == 2), zh, 1 - zh)

    def source(yh):
        return at(
            x_=jnp.where(u_own == rem(y, 2), x, rem(x + 2, 4)), y_=yh * 2 + div(zl, 2),
            zh_=half_of(zl), zl_=zh * 2 + div(y, 2),
        )

    def lanes_of(core):
        return pl.ds(pl.multiple_of(core * 1024, 1024), 1024)

    first = take(5)
    loads = [
        pltpu.make_async_copy(src, dst, sems.at[first + i])
        for i, (src, dst) in enumerate(
            ((ft_hbm, ft_ref), (list_hbm, list_ref), (count_hbm, count_ref), (inv_hbm, inv_ref),
             (a_ref, abuf.at[:, lanes_of(k)]))
        )
    ]
    for copy in loads:
        copy.start()

    barrier = pltpu.get_barrier_semaphore()

    def greet(device):
        pl.semaphore_signal(barrier, inc=1, device_id=device, device_id_type=MESH)

    greet(partner)
    for device in around_x:
        greet(device)
    for o in range(1, 8):
        greet(chip_t(rem(t + o, 8)))
    for o in range(1, 8):
        if o != 4:
            greet(chip_z(rem(z + o, 8)))

    for yh in range(2):
        s_row, s_col = source(yh)

        @pl.when((s_row != row) | (s_col != col))
        def _():
            greet((s_row, s_col))

    for copy in loads[:3]:
        copy.wait()

    s_iota = lax.broadcasted_iota(jnp.int32, (4, 128), 0)
    p_iota = lax.broadcasted_iota(jnp.int32, (4, 128), 1)
    counts = jnp.zeros((4, 128), jnp.int32)
    for s in range(4):
        counts = jnp.where(s_iota == s, count_ref[s], counts)
    listed = jnp.where(p_iota < counts, list_ref[...], -1)

    def live(tile):
        return jnp.max(jnp.where(listed == tile, 1.0, 0.0), axis=1, keepdims=True)

    for i in range(8):
        alive = live(row * 8 + i)
        for s in range(4):
            block = ft_ref[s, :, i * 128 : (i + 1) * 128]
            keep = jnp.broadcast_to(alive[s : s + 1, :], block.shape) > 0
            block = jnp.where(keep, block.astype(F32), 0.0).astype(BF16)
            fmask[s, :, i * 128 : (i + 1) * 128] = block
            ftile[i % 4, s, :, (i // 4) * 128 : (i // 4 + 1) * 128] = block
    alive = [live(row * 8 + half * 4 + y) for half in range(2)]

    pl.semaphore_wait(barrier, 19 - jnp.where(here, 1, 0))

    pending = []

    hop_send, hop_recv = take(2), take(2)
    kept = fmask.at[pl.ds(u_own * 2, 2)]
    given = fmask.at[pl.ds((1 - u_own) * 2, 2)]
    across = rem(x + 2, 4)
    gift = remote(
        given, fg.at[across, to_place, to_yh], hop_send + 1, hop_recv + to_yh,
        at(x_=across, y_=to_y, zh_=to_zh, zl_=to_place),
    )
    gift.start()
    pending.append(gift)
    there = fg.at[x, to_place, to_yh]
    local_kept = pltpu.make_async_copy(kept, there, sems.at[hop_recv + to_yh])
    remote_kept = remote(
        kept, there, hop_send, hop_recv + to_yh, at(y_=to_y, zh_=to_zh, zl_=to_place)
    )

    @pl.when(here)
    def _():
        local_kept.start()

    @pl.when(jnp.logical_not(here))
    def _():
        remote_kept.start()

    pending.append((jnp.logical_not(here), remote_kept))

    a_sems = take(2)
    a_swap = remote(a_ref, abuf.at[:, lanes_of(k)], a_sems, a_sems + 1, partner)
    a_swap.start()
    pending.append(a_swap)
    a_theirs = remote(a_ref, abuf.at[:, lanes_of(1 - k)], a_sems, a_sems + 1, partner)

    r_iota = lax.broadcasted_iota(jnp.int32, (256, 512), 0)
    c_iota = lax.broadcasted_iota(jnp.int32, (256, 512), 1)
    r_y = rem(div(r_iota, 64), 2) * 2 + div(r_iota, 128)
    r_s, r_w = rem(div(r_iota, 32), 2), rem(r_iota, 32)
    same_w = r_w == rem(c_iota, 32)
    for core in range(2):
        hit = same_w & (r_s == div(c_iota, 256)) & (div(rem(c_iota, 256), 32) == r_y * 2 + core)
        perm[core] = jnp.where(hit, 1.0, 0.0).astype(BF16)
    line_send, line_recv, pass_send = take(2), take(4), take(3)
    right_send, right_recv, left_send, left_recv = take(4), take(4), take(4), take(4)
    zh_at = [zh, 1 - zh]
    inner = (zl == 1) | (zl == 2)
    even = rem(zl, 2) == 0
    flip1 = jnp.where(even, zl + 1, zl - 1)
    flip2 = rem(zl + 2, 4)
    flip3 = 3 - zl
    order = [
        zl, jnp.where(inner, flip3, flip1), jnp.where(inner, flip1, flip2),
        jnp.where(inner, flip2, flip3),
    ]

    def along_line(place, sem, to):
        on = (to >= 0) & (to <= 3)
        block = fg.at[x, place]
        copy = remote(block, block, sem, line_recv + place, at(zl_=jnp.clip(to, 0, 3)))
        pl.when(on)(copy.start)
        pending.append((on, copy))

    def along_x(place):
        block = fg.at[x, place]
        for send, recv, device in (
            (right_send, right_recv, right), (left_send, left_recv, left)
        ):
            copy = remote(block, block, send + place, recv + place, device)
            copy.start()
            pending.append(copy)

    for yh in range(2):
        remote(
            kept, fg.at[x, zl, yh], hop_send, hop_recv + yh, around_x[0]
        ).wait_recv()
    along_line(zl, line_send, zl + 1)
    along_line(zl, line_send + 1, zl - 1)
    along_x(zl)
    def arrive_z(i):
        place = order[i]
        block = fg.at[x, place]
        remote(block, block, line_send, line_recv + place, around_x[0]).wait_recv()
        along_line(place, pass_send + i - 1, jnp.where(place > zl, zl - 1, zl + 1))
        along_x(place)

    fr_own_sem = take()
    fr_mine = pltpu.make_async_copy(ftile.at[y], fr.at[:, t, k], sems.at[fr_own_sem])
    fr_mine.start()
    fr_arrive = []

    def share_rows():
        for o in range(1, 8):
            t_to, t_from = rem(t + o, 8), rem(t + 8 - o, 8)
            send, recv = take(), take()
            copy = remote(ftile.at[rem(t_to, 4)], fr.at[:, t, k], send, recv, chip_t(t_to))
            copy.start()
            pending.append(copy)
            fr_arrive.append(
                remote(ftile.at[y], fr.at[:, t_from, k], send, recv, chip_t(t_from))
            )

    g_left, g_right, g_far = rem(x + 3, 4), rem(x + 1, 4), rem(x + 2, 4)
    far_right_send, far_right_recv = take(4), take(4)
    far_left_send, far_left_recv = take(4), take(4)

    def neighbours(i):
        place = order[i]
        for sems_at, group, half, onward, device, back in (
            ((right_send, right_recv), g_left, 0, (far_right_send, far_right_recv), right, left),
            ((left_send, left_recv), g_right, 1, (far_left_send, far_left_recv), left, right),
        ):
            block = fg.at[group, place]
            remote(block, block, sems_at[0] + place, sems_at[1] + place, back).wait_recv()
            part = fg.at[group, place, half]
            copy = remote(part, part, onward[0] + place, onward[1] + place, device)
            copy.start()
            pending.append(copy)

    def far(i):
        place = order[i]
        part = fg.at[g_far, place, 0]
        remote(part, part, far_right_send, far_right_recv + place, left).wait_recv()
        part = fg.at[g_far, place, 1]
        remote(part, part, far_left_send, far_left_recv + place, right).wait_recv()

    u_of = [u_own, 1 - u_own]
    b_of = [div(place, 2) for place in order]
    half_at = [half_of(place) for place in order]

    def partial(i, w):
        u, place, c = u_of[w], order[i], i * 2 + w

        block = jnp.concatenate(
            [fg[2 * u + h, place].reshape(128, 1024) for h in range(2)], axis=1
        )
        acc = lax.dot_general(abuf[...], block, NT_DIMS, preferred_element_type=F32)
        for j in range(8):
            pp[c, j // 4, j % 4] = acc[j * 128 : (j + 1) * 128].astype(BF16)
        for o in (2, 1, 3):
            sem = y_sems + (c * 3 + o - 1) * 2
            copy = remote(
                pp.at[c, :, rem(y + o, 4)], pyr.at[c, o - 1], sem, sem + 1, around_y[o - 1]
            )
            copy.start()
            pending.append(copy)

    y_sems = take(48)
    z_sems, c_sems = take(8), take(8)
    dy_send, dy_recv = take(8), take(8)
    dx_sems = take(24)
    dz_send, dz_recv = take(8), take(8)

    lane = lax.broadcasted_iota(jnp.int32, (1, 128), 1)
    lane_s = rem(div(lane, 32), 2)
    low = jnp.broadcast_to(lane, (512, 128)) < 64
    lane_live = []
    for w in range(2):
        for half in range(2):
            mask = jnp.zeros((1, 128), F32)
            for s in range(4):
                mask = jnp.where(lane_s + 2 * u_of[w] == s, alive[half][s : s + 1, :], mask)
            lane_live.append(mask)

    def reduce_y(i, w):
        c = i * 2 + w
        step = w * 2 + jnp.where(half_at[i] == zh, 0, 1)
        for o in (1, 3, 2):
            sem = y_sems + (c * 3 + o - 1) * 2
            came = around_y[3 - o]
            remote(pp.at[c, :, y], pyr.at[c, o - 1], sem, sem + 1, came).wait_recv()
        sums = []
        for half in range(2):
            acc = pp[c, half, y].astype(F32)
            for o in range(3):
                acc += pyr[c, o, half].astype(F32)
            acc = jnp.where(lane_live[w * 2 + half] > 0, acc, 0.0)
            for s in range(2):
                sb[i, u_of[w], s, half * 128 : (half + 1) * 128] = jnp.where(
                    lane_s == s, acc, 0.0
                ).astype(BF16)
            sums.append(acc)
        lanes = pl.ds(pl.multiple_of(b_of[i] * 128, 128), 128)
        zown[step, :, lanes] = jnp.where(zh == 0, sums[0], sums[1])
        zs[step, :, lanes] = jnp.where(zh == 0, sums[1], sums[0]).astype(BF16)

    def exchange(step):
        other = step + 1 - 2 * (step % 2)
        device = at(zh_=1 - zh)
        copy = remote(
            zs.at[step], zr.at[other], z_sems + step * 2, z_sems + other * 2 + 1, device
        )
        copy.start()
        pending.append(copy)
        return remote(
            zs.at[other], zr.at[step], z_sems + other * 2, z_sems + step * 2 + 1, device
        )

    def finish(step, z_copy):
        z_copy.wait_recv()
        pb[step] = (-(zown[step] + zr[step].astype(F32))).astype(BF16)
        theirs = pb.at[step, pl.ds(pl.multiple_of((1 - k) * 64, 64), 64)]
        copy = remote(theirs, cr.at[step], c_sems + step * 2, c_sems + step * 2 + 1, partner)
        copy.start()
        pending.append(copy)
        return copy

    def write_panel(step, c_copy):
        c_copy.wait_recv()
        mine = pb[step, pl.ds(pl.multiple_of(k * 64, 64), 64)]
        res = jnp.dot(mine, perm[k], preferred_element_type=F32)
        res += jnp.dot(cr[step], perm[1 - k], preferred_element_type=F32)
        for s in range(2):
            at_lane = (2 * u_of[step // 2] + s) * 512 + zh_at[step % 2] * 256
            panel_ref[:, pl.ds(pl.multiple_of(at_lane, 256), 256)] = res[
                :, s * 256 : (s + 1) * 256
            ].astype(BF16)

    def products(i):
        both = []
        for u in range(2):
            acc = jnp.zeros((512, 128), F32)
            for s in range(2):
                acc += jnp.dot(
                    fr[2 * u + s].reshape(512, 256), sb[i, u, s], preferred_element_type=F32
                )
            both.append(acc)
        turned = [pltpu.roll(acc, 64, 1) for acc in both]
        tiles = (jnp.where(low, both[0], turned[1]), jnp.where(low, turned[0], both[1]))
        for yh in range(2):
            for zl_ in range(4):
                for x_ in range(4):
                    first = zl_ * 128 + x_ * 32
                    dxs[i, x_, yh, zl_] = tiles[yh][first : first + 32].astype(BF16)
        for o in (2, 1, 3):
            sem = dx_sems + (i * 3 + o - 1) * 2
            copy = remote(
                dxs.at[i, rem(x + o, 4)], dxr.at[i, o - 1], sem, sem + 1, around_x[o - 1]
            )
            copy.start()
            pending.append(copy)

    def over_x(i):
        for o in (1, 3, 2):
            sem = dx_sems + (i * 3 + o - 1) * 2
            remote(
                dxs.at[i, x], dxr.at[i, o - 1], sem, sem + 1, around_x[3 - o]
            ).wait_recv()
        acc = dxs[i, x].astype(F32)
        for o in range(3):
            acc += dxr[i, o].astype(F32)
        dys[i] = acc.astype(BF16)
        half = half_at[i]
        for yh in range(2):
            y_to = yh * 2 + b_of[i]
            send = remote(
                dys.at[i, yh], dyr.at[half, y], dy_send + i * 2 + yh, dy_recv + half * 4 + y,
                at(y_=y_to),
            )
            pl.when(y_to != y)(send.start)
            pending.append((y_to != y, send))

            @pl.when(y_to == y)
            def _():
                dyr[half, y] = dys[i, yh]

    def over_y(j):
        half = zh_at[j]
        for o in (1, 3, 2):
            y_from = rem(y + o, 4)
            remote(
                dys.at[0, 0], dyr.at[half, y_from], dy_send, dy_recv + half * 4 + y_from,
                around_y[o - 1],
            ).wait_recv()
        acc = dyr[half, 0].astype(F32)
        for y_ in range(1, 4):
            acc += dyr[half, y_].astype(F32)
        dzs[j] = acc.astype(BF16)
        for o in (2, 1, 3, 0):
            zl_to = rem(zl + o, 4)
            if j == 0 and o == 0:
                dzr[z] = dzs[j, zl]
                continue
            copy = remote(
                dzs.at[j, zl_to], dzr.at[z], dz_send + j * 4 + o, dz_recv + z,
                at(zl_=zl_to, zh_=half),
            )
            copy.start()
            pending.append(copy)

    arrive_z(1)
    neighbours(0)
    loads[4].wait()
    a_theirs.wait_recv()
    partial(0, 0)
    arrive_z(2)
    neighbours(1)
    partial(1, 0)
    far(0)
    partial(0, 1)
    arrive_z(3)
    share_rows()
    neighbours(2)
    reduce_y(0, 0)
    partial(2, 0)
    far(1)
    partial(1, 1)
    reduce_y(1, 0)
    reduce_y(0, 1)
    neighbours(3)
    partial(3, 0)
    reduce_y(2, 0)
    reduce_y(1, 1)
    far(2)
    partial(2, 1)
    z0 = exchange(0)
    fr_mine.wait()
    for copy in fr_arrive:
        copy.wait_recv()
    fr_sems = take(2)
    fr_swap = remote(fr.at[:, :, k], fr.at[:, :, k], fr_sems, fr_sems + 1, partner)
    fr_swap.start()
    pending.append(fr_swap)
    far(3)
    partial(3, 1)
    reduce_y(3, 0)
    z1 = exchange(1)
    reduce_y(2, 1)
    z2 = exchange(2)
    remote(fr.at[:, :, 1 - k], fr.at[:, :, 1 - k], fr_sems, fr_sems + 1, partner).wait_recv()
    products(0)
    products(1)
    reduce_y(3, 1)
    products(2)
    products(3)
    z3 = exchange(3)
    over_x(0)
    over_x(1)
    c0 = finish(0, z0)
    over_x(2)
    c2 = finish(2, z2)
    over_y(0)
    c1 = finish(1, z1)
    over_x(3)
    write_panel(0, c0)
    write_panel(2, c2)
    over_y(1)
    c3 = finish(3, z3)
    write_panel(1, c1)
    write_panel(3, c3)
    for o in range(1, 8):
        z_from = rem(z + o, 8)
        remote(dzs.at[0, 0], dzr.at[z_from], dz_send, dz_recv + z_from, chip_z(z_from)).wait_recv()
    total = dzr[0].astype(F32)
    for z_ in range(1, 8):
        total += dzr[z_].astype(F32)
    loads[3].wait()
    for s in range(4):
        diag_ref[s] = inv_ref[s] + total[:, s * 32 : (s + 1) * 32]

    for copy in pending:
        if isinstance(copy, tuple):
            sent, copy = copy
            pl.when(sent)(copy.wait_send)
        else:
            copy.wait_send()
    assert used[0] <= SEMS, used


SEMS = 264


def per_device(inverse_tiles, factor, inverse_diag, tile_list, tile_count):
    vmem = pl.BlockSpec(memory_space=pltpu.VMEM)
    v = pltpu.VMEM
    panel, diag = pl.pallas_call(
        kernel,
        out_shape=(
            jax.ShapeDtypeStruct((64, 2048), BF16),
            jax.ShapeDtypeStruct((4, 32, 32), F32),
        ),
        in_specs=[pl.BlockSpec(memory_space=pl.ANY)] * 5,
        out_specs=(vmem, vmem),
        scratch_shapes=[
            v((4, 128), jnp.int32),
            pltpu.SMEM((4,), jnp.int32),
            v((4, 32, 1024), BF16),
            v((4, 32, 32), F32),
            v((1024, 2048), BF16),
            v((4, 32, 1024), BF16),
            v((4, 4, 32, 256), BF16),
            v((4, 4, 2, 2, 32, 1024), BF16),
            v((4, 8, 2, 32, 256), BF16),
            v((8, 2, 4, 128, 128), BF16),
            v((8, 3, 2, 128, 128), BF16),
            v((4, 2, 2, 256, 128), BF16),
            v((4, 128, 256), F32),
            v((4, 128, 256), BF16),
            v((4, 128, 256), BF16),
            v((4, 128, 256), BF16),
            v((4, 64, 256), BF16),
            v((4, 4, 2, 4, 32, 128), BF16),
            v((4, 3, 2, 4, 32, 128), BF16),
            v((4, 2, 4, 32, 128), BF16),
            v((2, 4, 4, 32, 128), BF16),
            v((2, 4, 32, 128), BF16),
            v((8, 32, 128), BF16),
            v((2, 256, 512), BF16),
            pltpu.SemaphoreType.DMA((SEMS,)),
        ],
        compiler_params=pltpu.CompilerParams(
            collective_id=0, has_side_effects=True, vmem_limit_bytes=60 * 1024 * 1024
        ),
        cost_estimate=pl.CostEstimate(
            flops=2 * 1024 * 2048 * 1024, bytes_accessed=4 << 20, transcendentals=0
        ),
    )(tile_list, tile_count, inverse_tiles, jnp.transpose(factor, (1, 2, 0)), inverse_diag)
    return panel.reshape(64, 4, 512), diag


def solution(mesh):
    return jax.shard_map(
        per_device,
        mesh=mesh,
        in_specs=(P("row", "col"), P("row", None, "col"), P(None, "row", "col"), P(), P()),
        out_specs=(P(("row", "col"), None, None), P(None, "row", "col")),
        check_vma=False,
    )
```

```python
import jax
import jax.numpy as jnp
from jax import lax
from jax.experimental import pallas as pl
from jax.experimental.pallas import tpu as pltpu
from jax.sharding import PartitionSpec as P

MESH = pl.DeviceIdType.MESH
F32 = jnp.float32
BF16 = jnp.bfloat16
NT_DIMS = (((1,), (1,)), ((), ()))


def div(a, b):
    return lax.div(a, jnp.int32(b))


def rem(a, b):
    return lax.rem(a, jnp.int32(b))


def kernel(
    list_hbm, count_hbm, a_ref, ft_hbm, inv_hbm, panel_ref, diag_ref,
    list_ref, count_ref, ft_ref, inv_ref,
    abuf, fmask, ftile, fg, fr, pp, pyr, sb, zown, zs, zr, pb, cr, dxs, dxr, dys, dyr, dzs,
    dzr, perm, sems,
):
    row, col = lax.axis_index("row"), lax.axis_index("col")
    zl, x = div(row, 4), rem(row, 4)
    zh, y, k = div(col, 8), rem(div(col, 2), 4), rem(col, 2)
    z, t = zh * 4 + zl, zh * 4 + y

    def at(zl_=zl, x_=x, zh_=zh, y_=y, k_=k):
        return (zl_ * 4 + x_, zh_ * 8 + y_ * 2 + k_)

    used = [0]

    def take(n=1):
        used[0] += n
        return used[0] - n

    def remote(src, dst, send, recv, device):
        return pltpu.make_async_remote_copy(
            src_ref=src, dst_ref=dst, send_sem=sems.at[send], recv_sem=sems.at[recv],
            device_id=device, device_id_type=MESH,
        )

    partner = at(k_=1 - k)
    around_x = [at(x_=rem(x + o, 4)) for o in (1, 2, 3)]
    around_y = [at(y_=rem(y + o, 4)) for o in (1, 2, 3)]
    right, left = around_x[0], around_x[2]

    def chip_t(t_):
        return at(zh_=div(t_, 4), y_=rem(t_, 4))

    def chip_z(z_, x_=x):
        return at(zh_=div(z_, 4), zl_=rem(z_, 4), x_=x_)

    u_own = div(x, 2)
    to_zh, to_y = div(zl, 2), rem(zl, 2) * 2 + div(x, 2)
    to_place = jnp.where(zh == to_zh, 1 + rem(y, 2), 3 * rem(y, 2))
    to_yh = div(y, 2)
    here = (to_zh == zh) & (to_y == y) & (to_place == zl)

    def half_of(place):
        return jnp.where((place == 1) | (place == 2), zh, 1 - zh)

    def source(yh):
        return at(
            x_=jnp.where(u_own == rem(y, 2), x, rem(x + 2, 4)), y_=yh * 2 + div(zl, 2),
            zh_=half_of(zl), zl_=zh * 2 + div(y, 2),
        )

    def lanes_of(core):
        return pl.ds(pl.multiple_of(core * 1024, 1024), 1024)

    first = take(5)
    loads = [
        pltpu.make_async_copy(src, dst, sems.at[first + i])
        for i, (src, dst) in enumerate(
            ((ft_hbm, ft_ref), (list_hbm, list_ref), (count_hbm, count_ref), (inv_hbm, inv_ref),
             (a_ref, abuf.at[:, lanes_of(k)]))
        )
    ]
    for copy in loads:
        copy.start()

    barrier = pltpu.get_barrier_semaphore()

    def greet(device):
        pl.semaphore_signal(barrier, inc=1, device_id=device, device_id_type=MESH)

    greet(partner)
    for device in around_x:
        greet(device)
    for o in range(1, 8):
        greet(chip_t(rem(t + o, 8)))
    for o in range(1, 8):
        if o != 4:
            greet(chip_z(rem(z + o, 8)))

    for yh in range(2):
        s_row, s_col = source(yh)

        @pl.when((s_row != row) | (s_col != col))
        def _():
            greet((s_row, s_col))

    for copy in loads[:3]:
        copy.wait()

    s_iota = lax.broadcasted_iota(jnp.int32, (4, 128), 0)
    p_iota = lax.broadcasted_iota(jnp.int32, (4, 128), 1)
    counts = jnp.zeros((4, 128), jnp.int32)
    for s in range(4):
        counts = jnp.where(s_iota == s, count_ref[s], counts)
    listed = jnp.where(p_iota < counts, list_ref[...], -1)

    def live(tile):
        return jnp.max(jnp.where(listed == tile, 1.0, 0.0), axis=1, keepdims=True)

    for i in range(8):
        alive = live(row * 8 + i)
        for s in range(4):
            block = ft_ref[s, :, i * 128 : (i + 1) * 128]
            keep = jnp.broadcast_to(alive[s : s + 1, :], block.shape) > 0
            block = jnp.where(keep, block.astype(F32), 0.0).astype(BF16)
            fmask[s, :, i * 128 : (i + 1) * 128] = block
            ftile[i % 4, s, :, (i // 4) * 128 : (i // 4 + 1) * 128] = block
    alive = [live(row * 8 + half * 4 + y) for half in range(2)]

    pl.semaphore_wait(barrier, 19 - jnp.where(here, 1, 0))

    pending = []

    hop_send, hop_recv = take(2), take(2)
    kept = fmask.at[pl.ds(u_own * 2, 2)]
    given = fmask.at[pl.ds((1 - u_own) * 2, 2)]
    across = rem(x + 2, 4)
    gift = remote(
        given, fg.at[across, to_place, to_yh], hop_send + 1, hop_recv + to_yh,
        at(x_=across, y_=to_y, zh_=to_zh, zl_=to_place),
    )
    gift.start()
    pending.append(gift)
    there = fg.at[x, to_place, to_yh]
    local_kept = pltpu.make_async_copy(kept, there, sems.at[hop_recv + to_yh])
    remote_kept = remote(
        kept, there, hop_send, hop_recv + to_yh, at(y_=to_y, zh_=to_zh, zl_=to_place)
    )

    @pl.when(here)
    def _():
        local_kept.start()

    @pl.when(jnp.logical_not(here))
    def _():
        remote_kept.start()

    pending.append((jnp.logical_not(here), remote_kept))

    a_sems = take(2)
    a_swap = remote(a_ref, abuf.at[:, lanes_of(k)], a_sems, a_sems + 1, partner)
    a_swap.start()
    pending.append(a_swap)
    a_theirs = remote(a_ref, abuf.at[:, lanes_of(1 - k)], a_sems, a_sems + 1, partner)

    r_iota = lax.broadcasted_iota(jnp.int32, (256, 512), 0)
    c_iota = lax.broadcasted_iota(jnp.int32, (256, 512), 1)
    r_y = rem(div(r_iota, 64), 2) * 2 + div(r_iota, 128)
    r_s, r_w = rem(div(r_iota, 32), 2), rem(r_iota, 32)
    same_w = r_w == rem(c_iota, 32)
    for core in range(2):
        hit = same_w & (r_s == div(c_iota, 256)) & (div(rem(c_iota, 256), 32) == r_y * 2 + core)
        perm[core] = jnp.where(hit, 1.0, 0.0).astype(BF16)
    line_send, line_recv, pass_send = take(2), take(4), take(3)
    right_send, right_recv, left_send, left_recv = take(4), take(4), take(4), take(4)
    zh_at = [zh, 1 - zh]
    inner = (zl == 1) | (zl == 2)
    even = rem(zl, 2) == 0
    flip1 = jnp.where(even, zl + 1, zl - 1)
    flip2 = rem(zl + 2, 4)
    flip3 = 3 - zl
    order = [
        zl, jnp.where(inner, flip3, flip1), jnp.where(inner, flip1, flip2),
        jnp.where(inner, flip2, flip3),
    ]

    def along_line(place, sem, to):
        on = (to >= 0) & (to <= 3)
        block = fg.at[x, place]
        copy = remote(block, block, sem, line_recv + place, at(zl_=jnp.clip(to, 0, 3)))
        pl.when(on)(copy.start)
        pending.append((on, copy))

    def along_x(place):
        block = fg.at[x, place]
        for send, recv, device in (
            (right_send, right_recv, right), (left_send, left_recv, left)
        ):
            copy = remote(block, block, send + place, recv + place, device)
            copy.start()
            pending.append(copy)

    for yh in range(2):
        remote(
            kept, fg.at[x, zl, yh], hop_send, hop_recv + yh, around_x[0]
        ).wait_recv()
    along_line(zl, line_send, zl + 1)
    along_line(zl, line_send + 1, zl - 1)
    along_x(zl)
    def arrive_z(i):
        place = order[i]
        block = fg.at[x, place]
        remote(block, block, line_send, line_recv + place, around_x[0]).wait_recv()
        along_line(place, pass_send + i - 1, jnp.where(place > zl, zl - 1, zl + 1))
        along_x(place)

    fr_own_sem = take()
    fr_mine = pltpu.make_async_copy(ftile.at[y], fr.at[:, t, k], sems.at[fr_own_sem])
    fr_mine.start()
    fr_arrive = []

    def share_rows():
        for o in range(1, 8):
            t_to, t_from = rem(t + o, 8), rem(t + 8 - o, 8)
            send, recv = take(), take()
            copy = remote(ftile.at[rem(t_to, 4)], fr.at[:, t, k], send, recv, chip_t(t_to))
            copy.start()
            pending.append(copy)
            fr_arrive.append(
                remote(ftile.at[y], fr.at[:, t_from, k], send, recv, chip_t(t_from))
            )

    g_left, g_right, g_far = rem(x + 3, 4), rem(x + 1, 4), rem(x + 2, 4)
    far_right_send, far_right_recv = take(4), take(4)
    far_left_send, far_left_recv = take(4), take(4)

    def neighbours(i):
        place = order[i]
        for sems_at, group, half, onward, device, back in (
            ((right_send, right_recv), g_left, 0, (far_right_send, far_right_recv), right, left),
            ((left_send, left_recv), g_right, 1, (far_left_send, far_left_recv), left, right),
        ):
            block = fg.at[group, place]
            remote(block, block, sems_at[0] + place, sems_at[1] + place, back).wait_recv()
            part = fg.at[group, place, half]
            copy = remote(part, part, onward[0] + place, onward[1] + place, device)
            copy.start()
            pending.append(copy)

    def far(i):
        place = order[i]
        part = fg.at[g_far, place, 0]
        remote(part, part, far_right_send, far_right_recv + place, left).wait_recv()
        part = fg.at[g_far, place, 1]
        remote(part, part, far_left_send, far_left_recv + place, right).wait_recv()

    u_of = [u_own, 1 - u_own]
    b_of = [div(place, 2) for place in order]
    half_at = [half_of(place) for place in order]

    def partial(i, w):
        u, place, c = u_of[w], order[i], i * 2 + w

        block = jnp.concatenate(
            [fg[2 * u + h, place].reshape(128, 1024) for h in range(2)], axis=1
        )
        acc = lax.dot_general(abuf[...], block, NT_DIMS, preferred_element_type=F32)
        for j in range(8):
            pp[c, j // 4, j % 4] = acc[j * 128 : (j + 1) * 128].astype(BF16)
        for o in (2, 1, 3):
            sem = y_sems + (c * 3 + o - 1) * 2
            copy = remote(
                pp.at[c, :, rem(y + o, 4)], pyr.at[c, o - 1], sem, sem + 1, around_y[o - 1]
            )
            copy.start()
            pending.append(copy)

    y_sems = take(48)
    z_sems, c_sems = take(8), take(8)
    dy_send, dy_recv = take(8), take(8)
    dx_sems = take(24)
    dz_send, dz_recv = take(8), take(8)

    lane = lax.broadcasted_iota(jnp.int32, (1, 128), 1)
    lane_s = rem(div(lane, 32), 2)
    low = jnp.broadcast_to(lane, (512, 128)) < 64
    lane_live = []
    for w in range(2):
        for half in range(2):
            mask = jnp.zeros((1, 128), F32)
            for s in range(4):
                mask = jnp.where(lane_s + 2 * u_of[w] == s, alive[half][s : s + 1, :], mask)
            lane_live.append(mask)

    def reduce_y(i, w):
        c = i * 2 + w
        step = w * 2 + jnp.where(half_at[i] == zh, 0, 1)
        for o in (1, 3, 2):
            sem = y_sems + (c * 3 + o - 1) * 2
            came = around_y[3 - o]
            remote(pp.at[c, :, y], pyr.at[c, o - 1], sem, sem + 1, came).wait_recv()
        sums = []
        for half in range(2):
            acc = pp[c, half, y].astype(F32)
            for o in range(3):
                acc += pyr[c, o, half].astype(F32)
            acc = jnp.where(lane_live[w * 2 + half] > 0, acc, 0.0)
            for s in range(2):
                sb[i, u_of[w], s, half * 128 : (half + 1) * 128] = jnp.where(
                    lane_s == s, acc, 0.0
                ).astype(BF16)
            sums.append(acc)
        lanes = pl.ds(pl.multiple_of(b_of[i] * 128, 128), 128)
        zown[step, :, lanes] = jnp.where(zh == 0, sums[0], sums[1])
        zs[step, :, lanes] = jnp.where(zh == 0, sums[1], sums[0]).astype(BF16)

    def exchange(step):
        other = step + 1 - 2 * (step % 2)
        device = at(zh_=1 - zh)
        copy = remote(
            zs.at[step], zr.at[other], z_sems + step * 2, z_sems + other * 2 + 1, device
        )
        copy.start()
        pending.append(copy)
        return remote(
            zs.at[other], zr.at[step], z_sems + other * 2, z_sems + step * 2 + 1, device
        )

    def finish(step, z_copy):
        z_copy.wait_recv()
        pb[step] = (-(zown[step] + zr[step].astype(F32))).astype(BF16)
        theirs = pb.at[step, pl.ds(pl.multiple_of((1 - k) * 64, 64), 64)]
        copy = remote(theirs, cr.at[step], c_sems + step * 2, c_sems + step * 2 + 1, partner)
        copy.start()
        pending.append(copy)
        return copy

    def write_panel(step, c_copy):
        c_copy.wait_recv()
        mine = pb[step, pl.ds(pl.multiple_of(k * 64, 64), 64)]
        res = jnp.dot(mine, perm[k], preferred_element_type=F32)
        res += jnp.dot(cr[step], perm[1 - k], preferred_element_type=F32)
        for s in range(2):
            at_lane = (2 * u_of[step // 2] + s) * 512 + zh_at[step % 2] * 256
            panel_ref[:, pl.ds(pl.multiple_of(at_lane, 256), 256)] = res[
                :, s * 256 : (s + 1) * 256
            ].astype(BF16)

    def products(i):
        both = []
        for u in range(2):
            acc = jnp.zeros((512, 128), F32)
            for s in range(2):
                acc += jnp.dot(
                    fr[2 * u + s].reshape(512, 256), sb[i, u, s], preferred_element_type=F32
                )
            both.append(acc)
        turned = [pltpu.roll(acc, 64, 1) for acc in both]
        tiles = (jnp.where(low, both[0], turned[1]), jnp.where(low, turned[0], both[1]))
        for yh in range(2):
            for zl_ in range(4):
                for x_ in range(4):
                    first = zl_ * 128 + x_ * 32
                    dxs[i, x_, yh, zl_] = tiles[yh][first : first + 32].astype(BF16)
        for o in (2, 1, 3):
            sem = dx_sems + (i * 3 + o - 1) * 2
            copy = remote(
                dxs.at[i, rem(x + o, 4)], dxr.at[i, o - 1], sem, sem + 1, around_x[o - 1]
            )
            copy.start()
            pending.append(copy)

    def over_x(i):
        for o in (1, 3, 2):
            sem = dx_sems + (i * 3 + o - 1) * 2
            remote(
                dxs.at[i, x], dxr.at[i, o - 1], sem, sem + 1, around_x[3 - o]
            ).wait_recv()
        acc = dxs[i, x].astype(F32)
        for o in range(3):
            acc += dxr[i, o].astype(F32)
        dys[i] = acc.astype(BF16)
        half = half_at[i]
        for yh in range(2):
            y_to = yh * 2 + b_of[i]
            send = remote(
                dys.at[i, yh], dyr.at[half, y], dy_send + i * 2 + yh, dy_recv + half * 4 + y,
                at(y_=y_to),
            )
            pl.when(y_to != y)(send.start)
            pending.append((y_to != y, send))

            @pl.when(y_to == y)
            def _():
                dyr[half, y] = dys[i, yh]

    def over_y(j):
        half = zh_at[j]
        for o in (1, 3, 2):
            y_from = rem(y + o, 4)
            remote(
                dys.at[0, 0], dyr.at[half, y_from], dy_send, dy_recv + half * 4 + y_from,
                around_y[o - 1],
            ).wait_recv()
        acc = dyr[half, 0].astype(F32)
        for y_ in range(1, 4):
            acc += dyr[half, y_].astype(F32)
        dzs[j] = acc.astype(BF16)
        for o in (2, 1, 3, 0):
            zl_to = rem(zl + o, 4)
            if j == 0 and o == 0:
                dzr[z] = dzs[j, zl]
                continue
            copy = remote(
                dzs.at[j, zl_to], dzr.at[z], dz_send + j * 4 + o, dz_recv + z,
                at(zl_=zl_to, zh_=half),
            )
            copy.start()
            pending.append(copy)

    arrive_z(1)
    neighbours(0)
    loads[4].wait()
    a_theirs.wait_recv()
    partial(0, 0)
    arrive_z(2)
    neighbours(1)
    partial(1, 0)
    arrive_z(3)
    far(0)
    partial(0, 1)
    share_rows()
    neighbours(2)
    reduce_y(0, 0)
    partial(2, 0)
    far(1)
    partial(1, 1)
    reduce_y(1, 0)
    reduce_y(0, 1)
    neighbours(3)
    partial(3, 0)
    reduce_y(2, 0)
    reduce_y(1, 1)
    far(2)
    partial(2, 1)
    z0 = exchange(0)
    fr_mine.wait()
    for copy in fr_arrive:
        copy.wait_recv()
    fr_sems = take(2)
    fr_swap = remote(fr.at[:, :, k], fr.at[:, :, k], fr_sems, fr_sems + 1, partner)
    fr_swap.start()
    pending.append(fr_swap)
    far(3)
    partial(3, 1)
    reduce_y(3, 0)
    z1 = exchange(1)
    reduce_y(2, 1)
    z2 = exchange(2)
    remote(fr.at[:, :, 1 - k], fr.at[:, :, 1 - k], fr_sems, fr_sems + 1, partner).wait_recv()
    products(0)
    products(1)
    reduce_y(3, 1)
    products(2)
    products(3)
    z3 = exchange(3)
    over_x(0)
    over_x(1)
    c0 = finish(0, z0)
    over_x(2)
    c2 = finish(2, z2)
    over_y(0)
    c1 = finish(1, z1)
    over_x(3)
    write_panel(0, c0)
    write_panel(2, c2)
    over_y(1)
    c3 = finish(3, z3)
    write_panel(1, c1)
    write_panel(3, c3)
    for o in range(1, 8):
        z_from = rem(z + o, 8)
        remote(dzs.at[0, 0], dzr.at[z_from], dz_send, dz_recv + z_from, chip_z(z_from)).wait_recv()
    total = dzr[0].astype(F32)
    for z_ in range(1, 8):
        total += dzr[z_].astype(F32)
    loads[3].wait()
    for s in range(4):
        diag_ref[s] = inv_ref[s] + total[:, s * 32 : (s + 1) * 32]

    for copy in pending:
        if isinstance(copy, tuple):
            sent, copy = copy
            pl.when(sent)(copy.wait_send)
        else:
            copy.wait_send()
    assert used[0] <= SEMS, used


SEMS = 264


def per_device(inverse_tiles, factor, inverse_diag, tile_list, tile_count):
    vmem = pl.BlockSpec(memory_space=pltpu.VMEM)
    v = pltpu.VMEM
    panel, diag = pl.pallas_call(
        kernel,
        out_shape=(
            jax.ShapeDtypeStruct((64, 2048), BF16),
            jax.ShapeDtypeStruct((4, 32, 32), F32),
        ),
        in_specs=[pl.BlockSpec(memory_space=pl.ANY)] * 5,
        out_specs=(vmem, vmem),
        scratch_shapes=[
            v((4, 128), jnp.int32),
            pltpu.SMEM((4,), jnp.int32),
            v((4, 32, 1024), BF16),
            v((4, 32, 32), F32),
            v((1024, 2048), BF16),
            v((4, 32, 1024), BF16),
            v((4, 4, 32, 256), BF16),
            v((4, 4, 2, 2, 32, 1024), BF16),
            v((4, 8, 2, 32, 256), BF16),
            v((8, 2, 4, 128, 128), BF16),
            v((8, 3, 2, 128, 128), BF16),
            v((4, 2, 2, 256, 128), BF16),
            v((4, 128, 256), F32),
            v((4, 128, 256), BF16),
            v((4, 128, 256), BF16),
            v((4, 128, 256), BF16),
            v((4, 64, 256), BF16),
            v((4, 4, 2, 4, 32, 128), BF16),
            v((4, 3, 2, 4, 32, 128), BF16),
            v((4, 2, 4, 32, 128), BF16),
            v((2, 4, 4, 32, 128), BF16),
            v((2, 4, 32, 128), BF16),
            v((8, 32, 128), BF16),
            v((2, 256, 512), BF16),
            pltpu.SemaphoreType.DMA((SEMS,)),
        ],
        compiler_params=pltpu.CompilerParams(
            collective_id=0, has_side_effects=True, vmem_limit_bytes=60 * 1024 * 1024
        ),
        cost_estimate=pl.CostEstimate(
            flops=2 * 1024 * 2048 * 1024, bytes_accessed=4 << 20, transcendentals=0
        ),
    )(tile_list, tile_count, inverse_tiles, jnp.transpose(factor, (1, 2, 0)), inverse_diag)
    return panel.reshape(64, 4, 512), diag


def solution(mesh):
    return jax.shard_map(
        per_device,
        mesh=mesh,
        in_specs=(P("row", "col"), P("row", None, "col"), P(None, "row", "col"), P(), P()),
        out_specs=(P(("row", "col"), None, None), P(None, "row", "col")),
        check_vma=False,
    )
```
